1024 devices in a mesh: src: 4 (over x), space: 256 (over y, z, core).
Axes of the slice: x: 4, y: 4, z: 32, core: 2. Of those that a mesh axis runs over, the one named last changes fastest.
Arguments:
- adjoint_source: float32 [4, 6, 1024, 64, 128], P('src', None, 'space'), may hold values from -6 to 6
- forward_field: bfloat16 [4, 6, 1024, 64, 128], P('src', None, 'space'), may hold values from -6 to 6
- medium: float32 [2, 1024, 64, 128], P(None, 'space'), may hold values from 0.3 to 3
- plane_map: int32 [1024, 64], P('space'), may hold values from 0 to 255, as said below
- depth: int32 [4, 1024, 64], P('src', 'space'), may hold values from 1 to 128
- rough: float32 [9, 256, 32, 128], P(None, 'space'), may hold values from 0.2 to 1
Outputs:
- gradient: float32 [256, 32, 128], P('space')
The draws below stay inside these ranges and needn't reach their ends.
Inputs may be any that keep to these rules, and one draw needn't show every extreme that they name: plane_map[x, y] differs from x // 4 by at most 2.
All inputs are finite; a program needn't handle non-finite values.
Results may differ from the reference program's by a relative error of at most 0.0003.
Values sent between devices are 32-bit elements; how exact they have to be, the bound alone decides.
A program may use at most 32 MiB of HBM per device.

```python
import math
import jax
import jax.numpy as jnp
from jax import lax

CX = 4
NY = 64
NZ = 128
SWEEPS = 4
REACH = 2
SOURCES = 4
NX = 1024
IX = 256
IY = 32


def draw_plane_map(key, part):
    column = lax.iota(jnp.int32, NY)[None, :]
    base = (lax.iota(jnp.int32, NX) // CX)[:, None]
    jitter = jax.random.randint(key, (NX, NY), -REACH, REACH + 1)
    jitter = jnp.where(column == 0, REACH, jnp.where(column == 1, -REACH, jitter))
    return jnp.clip(base + jitter, 0, IX - 1).astype(jnp.int32)


def touch_ends(entries, own_key, smallest, largest):
    place = [jax.random.randint(jax.random.fold_in(own_key, axis), (), 0, length) for axis, length in enumerate(entries.shape)]
    longest = entries.shape.index(max(entries.shape))
    neighbour = place[:longest] + [(place[longest] + 1) % entries.shape[longest]] + place[longest + 1:]
    return entries.at[tuple(place)].set(smallest).at[tuple(neighbour)].set(largest)


def levels(key, dims, shards, low, largest):
    level = 1.0
    for axis_at, parts in shards:
        steps = jax.random.uniform(jax.random.fold_in(jax.random.fold_in(key, 6), axis_at), (parts,), jnp.float32, low / len(shards), largest / len(shards))
        level = level * jnp.repeat(jnp.exp(steps), dims[axis_at] // parts).reshape((-1,) + (1,) * (len(dims) - 1 - axis_at))
    return level


def centred(stream_key, shape, deviation, most, cuts=(), kind=jnp.bfloat16):
    level = levels(stream_key, shape, cuts, -0.22, 0.18) if cuts else 1.0
    array = jax.random.normal(stream_key, shape, jnp.float32) * deviation * level
    return jnp.minimum(jnp.maximum(array, -most), most).astype(kind)


def setup_inputs(seed: int = 0) -> dict:
    key_list = jax.random.split(jax.random.key(seed), 7)
    return {
        "adjoint_source": centred(key_list[0], (SOURCES, 6, NX, NY, NZ), 1.0, 6.0, ((0, 4), (2, 256)), jnp.float32),
        "forward_field": centred(key_list[1], (SOURCES, 6, NX, NY, NZ), 1.0, 6.0, ((0, 4), (2, 256))),
        "medium": jnp.clip(jnp.exp(math.log(3.0) - 2.3025851 * jax.random.uniform(key_list[2], (2, NX, NY, NZ), jnp.float32) ** levels(key_list[2], (2, NX, NY, NZ), ((1, 256),), -0.2, 0.2)), 0.3, 3.0),
        "plane_map": draw_plane_map(jax.random.fold_in(key_list[6], 71), 0),
        "depth": touch_ends(jax.random.randint(key_list[4], (SOURCES, NX, NY), 1, NZ + 1), jax.random.fold_in(key_list[4], 1), 1, NZ).astype(jnp.int32),
        "rough": jnp.clip(jnp.exp(math.log(1.0) - 1.609438 * jax.random.uniform(key_list[5], (9, IX, IY, NZ), jnp.float32) ** levels(key_list[5], (9, IX, IY, NZ), ((1, 256),), -0.2, 0.2)), 0.2, 1.0),
    }


sweep_steps = (0.323, 1.658, 0.422, 0.752)


def ahead_rows(value):
    return jnp.concatenate([value[..., 1:, :], jnp.zeros_like(value[..., :1, :])], axis=-2)


def ahead_depth(value):
    return jnp.concatenate([value[..., 1:], jnp.zeros_like(value[..., :1])], axis=-1)


def behind_rows(value):
    return jnp.concatenate([jnp.zeros_like(value[..., :1, :]), value[..., :-1, :]], axis=-2) - value


def behind_depth(value):
    return jnp.concatenate([jnp.zeros_like(value[..., :1]), value[..., :-1]], axis=-1) - value


def lower_planes(value):
    return value[..., :-1, :, :]


def upper_planes(value):
    return value[..., 1:, :, :]


def step_planes(value):
    return value[..., 1:, :, :] - value[..., :-1, :, :]


def back_planes(value):
    return value[..., :-1, :, :] - value[..., 1:, :, :]


def curl_curl(padded, inside):
    shape = padded.shape
    planes = shape[-3]
    split = padded.reshape(shape[:-4] + (2, 3) + shape[-3:])
    field_x = split[..., 0, :, :, :]
    field_y = split[..., 1, :, :, :]
    field_z = split[..., 2, :, :, :]
    front = inside[:-1][:, None, None]
    curl_x = (ahead_rows(lower_planes(field_z)) - lower_planes(field_z)) - (ahead_depth(lower_planes(field_y)) - lower_planes(field_y))
    curl_y = (ahead_depth(lower_planes(field_x)) - lower_planes(field_x)) - step_planes(field_z)
    curl_z = step_planes(field_y) - (ahead_rows(lower_planes(field_x)) - lower_planes(field_x))
    curl_x = curl_x * front
    curl_y = curl_y * front
    curl_z = curl_z * front
    out_x = behind_depth(upper_planes(curl_y)) - behind_rows(upper_planes(curl_z))
    out_y = back_planes(curl_z) - behind_depth(upper_planes(curl_x))
    out_z = behind_rows(upper_planes(curl_x)) - back_planes(curl_y)
    stacked = jnp.stack([out_x, out_y, out_z], axis=-4)
    return stacked.reshape(shape[:-4] + (6, planes - 2) + shape[-2:])


def sweep(padded, source, mass_real, mass_imag, inside, weight):
    image = curl_curl(padded, inside)
    center = padded[..., 1:-1, :, :]
    real_part = center[..., 0:3, :, :, :]
    imag_part = center[..., 3:6, :, :, :]
    applied = jnp.concatenate([
        image[..., 0:3, :, :, :] + mass_real * real_part - mass_imag * imag_part,
        image[..., 3:6, :, :, :] + mass_real * imag_part + mass_imag * real_part], axis=-4)
    residual = source - applied
    diagonal = 4.0 + mass_real
    return (center + weight * residual / diagonal) * inside[1:-1][:, None, None]


def edge_parts(adjoint, saved):
    saved_wide = saved.astype(jnp.float32)
    moment = saved_wide[..., 0:3, :, :, :] * adjoint[..., 3:6, :, :, :] + saved_wide[..., 3:6, :, :, :] * adjoint[..., 0:3, :, :, :]
    moment_x = moment[..., 0, :, :, :]
    moment_y = moment[..., 1, :, :, :]
    moment_z = moment[..., 2, :, :, :]
    part_x = moment_x + ahead_depth(moment_x)
    part_x = part_x + ahead_rows(part_x)
    part_y = moment_y + ahead_depth(moment_y)
    part_z = moment_z + ahead_rows(moment_z)
    return part_x, part_y, part_z


def transposed_smooth(summed, rough):
    rows_in = summed.shape[-2]
    depth_in = summed.shape[-1]
    total = jnp.zeros_like(summed)
    for vertical in range(3):
        for lateral in range(3):
            product = rough[vertical * 3 + lateral] * summed
            padded = jnp.pad(product, ((0, 0), (1, 1), (1, 1)))
            total = total + padded[:, 2 - vertical:2 - vertical + rows_in, 2 - lateral:2 - lateral + depth_in]
    return total


def reference(adjoint_source, forward_field, medium, plane_map, depth, rough):
    mass_real = medium[0][None]
    mass_imag = medium[1][None]
    inside = jnp.concatenate([jnp.zeros((1,), jnp.float32), jnp.ones((NX,), jnp.float32), jnp.zeros((1,), jnp.float32)])

    def one_source(group):
        source, saved, level = group
        adjoint = sweep_steps[0] * source / (4.0 + mass_real)
        for sweep_index in range(1, SWEEPS):
            padded = jnp.pad(adjoint, ((0, 0), (1, 1), (0, 0), (0, 0)))
            adjoint = sweep(padded, source, mass_real, mass_imag, inside, sweep_steps[sweep_index])
        part_x, part_y, part_z = edge_parts(adjoint, saved)
        next_y = jnp.concatenate([part_y[1:], jnp.zeros_like(part_y[:1])], axis=0)
        next_z = jnp.concatenate([part_z[1:], jnp.zeros_like(part_z[:1])], axis=0)
        cell = 0.25 * (part_x + (part_y + next_y) + (part_z + next_z))
        keep = (lax.iota(jnp.int32, NZ)[None, None, :] < level[:, :, None]).astype(jnp.float32)
        return cell * keep

    cells = lax.map(one_source, (adjoint_source, forward_field, depth))
    local = jnp.sum(cells, axis=0)
    segment = (plane_map * IY + (lax.iota(jnp.int32, NY) // 2)[None, :]).astype(jnp.int32)
    summed = jax.ops.segment_sum(local.reshape(NX * NY, NZ), segment.reshape(NX * NY), num_segments=IX * IY)
    summed = summed.reshape(IX, IY, NZ)
    return transposed_smooth(summed, rough)
```

```python
import functools

import jax
import jax.numpy as jnp
from jax import lax
from jax.experimental import pallas as pl
from jax.experimental.pallas import tpu as pltpu
from jax.sharding import PartitionSpec as P

MESH = pl.DeviceIdType.MESH
SWEEPS = 4
REACH = 2
STEPS = (0.323, 1.658, 0.422, 0.752)
PAD = 8
BLOCK = 16
LOW, HIGH = -REACH - 1, REACH


def kernel(
    groups, count,
    source_hbm, saved_hbm, medium_hbm, map_hbm, depth_hbm, rough_hbm,
    out_ref,
    source, saved, mass, plane_map, depth, rough,
    inverse, field, mixed, part, upper, lower, where_to, how_deep, edge_out, edge_in,
    window, sent, landed, total, shares, padded,
    source_sem, mass_sem, load_sem, halo_send, halo_recv, edge_sem, window_send, window_recv, share_send, share_recv,
):
    planes, rows, cells = source.shape[1:]
    group = lax.axis_index("src")
    me = lax.axis_index("space")
    core = lax.rem(me, 2)
    has_below, has_above = me > 0, me < count - 1
    blocks = range(0, rows, BLOCK)
    lane = lax.broadcasted_iota(jnp.int32, (BLOCK, cells), 1)
    first_lane, last_lane = lane == 0, lane == cells - 1

    def at(start):
        return pl.ds(PAD + start, BLOCK)

    def ahead(value):
        return jnp.where(last_lane, 0.0, pltpu.roll(value, cells - 1, 1))

    def behind(value):
        return jnp.where(first_lane, 0.0, pltpu.roll(value, 1, 1))

    def present(offset):
        other = me + offset
        return (other >= 0) & (other < count)

    barrier = pltpu.get_barrier_semaphore()
    awaited = groups - 1
    for offset in (1, -1, 2, -2, 3):
        @pl.when(present(offset))
        def _():
            pl.semaphore_signal(barrier, inc=1, device_id={"space": me + offset}, device_id_type=MESH)
    for offset in range(1, groups):
        pl.semaphore_signal(barrier, inc=1, device_id={"src": lax.rem(group + offset, groups)}, device_id_type=MESH)
    for offset in range(LOW, HIGH + 1):
        if offset != 0:
            awaited = awaited + present(offset).astype(jnp.int32)

    def load_source(p):
        return pltpu.make_async_copy(source_hbm.at[0, :, p], source.at[:, p], source_sem.at[p])

    def load_mass(p):
        return pltpu.make_async_copy(medium_hbm.at[:, p], mass.at[:, p], mass_sem.at[p])

    for p in (0, planes - 1, *range(1, planes - 1)):
        load_source(p).start()
        load_mass(p).start()
    load_depth = pltpu.make_async_copy(depth_hbm.at[0], depth, load_sem.at[0])
    load_map = pltpu.make_async_copy(map_hbm, plane_map, load_sem.at[1])
    load_saved = pltpu.make_async_copy(saved_hbm.at[0], saved, load_sem.at[2])
    load_rough = pltpu.make_async_copy(rough_hbm.at[:, 0], rough, load_sem.at[3])
    for load in (load_depth, load_map, load_saved, load_rough):
        load.start()

    margin = jnp.zeros((PAD, cells), jnp.float32)
    for k in range(SWEEPS - 1):
        for p in range(planes):
            for c in (0, 1, 4, 5):
                field[k, p, c, pl.ds(PAD + rows, PAD), :] = margin
            for c in (2, 3):
                field[k, p + 1, c, pl.ds(0, PAD), :] = margin
                mixed[k, p + 1, c, pl.ds(0, PAD), :] = margin
            for c in (4, 5):
                mixed[k, p + 1, c, pl.ds(0, PAD), :] = margin
    for c in (0, 1):
        part[c, pl.ds(PAD + rows, PAD), :] = margin
    padded[...] = jnp.zeros_like(padded)

    @pl.when(jnp.logical_not(has_below))
    def _():
        for k in range(SWEEPS - 1):
            mixed[k, 0] = jnp.zeros(mixed.shape[2:], jnp.float32)
        edge_in[...] = jnp.full(edge_in.shape, -1000.0, jnp.float32)

    @pl.when(jnp.logical_not(has_above))
    def _():
        for k in range(SWEEPS - 1):
            field[k, planes, 2:6] = jnp.zeros((4, *field.shape[3:]), jnp.float32)

    def halo_down(k):
        return pltpu.make_async_remote_copy(
            src_ref=field.at[k, 0, 2:6, PAD:PAD + rows],
            dst_ref=field.at[k, planes, 2:6, PAD:PAD + rows],
            send_sem=halo_send.at[k, 0],
            recv_sem=halo_recv.at[k, 0],
            device_id={"space": me - 1},
            device_id_type=MESH,
        )

    def halo_up(k):
        return pltpu.make_async_remote_copy(
            src_ref=mixed.at[k, planes, 0:4, PAD:PAD + rows],
            dst_ref=mixed.at[k, 0, 0:4, PAD:PAD + rows],
            send_sem=halo_send.at[k, 1],
            recv_sem=halo_recv.at[k, 1],
            device_id={"space": me + 1},
            device_id_type=MESH,
        )

    edge_up = pltpu.make_async_remote_copy(
        src_ref=edge_out,
        dst_ref=edge_in,
        send_sem=edge_sem.at[0],
        recv_sem=edge_sem.at[1],
        device_id={"space": me + 1},
        device_id_type=MESH,
    )

    def combine(k, p):
        for r in blocks:
            for i in (0, 1):
                x, y, z = (field[k, p, 2 * c + i, at(r), :] for c in range(3))
                x_next, z_next = (field[k, p, 2 * c + i, at(r + 1), :] for c in (0, 2))
                mixed[k, p + 1, i, at(r), :] = (ahead(x) - x) + z
                mixed[k, p + 1, 2 + i, at(r), :] = y + (x_next - x)
                mixed[k, p + 1, 4 + i, at(r), :] = (z_next - z) - (ahead(y) - y)

    def begin(p):
        load_source(p).wait()
        load_mass(p).wait()
        for r in blocks:
            span = pl.ds(r, BLOCK)
            turned = 1.0 / (4.0 + mass[0, p, span, :])
            inverse[p, span, :] = turned
            turned = STEPS[0] * turned
            for c in range(3):
                for i in (0, 1):
                    field[0, p, 2 * c + i, at(r), :] = source[c + 3 * i, p, span, :] * turned
        combine(0, p)

    def update(k, p, weight):
        before = k - 1
        inside = jnp.where((me == 0) & (p == 0), 0.0, 1.0).astype(jnp.float32)
        for r in blocks:
            span = pl.ds(r, BLOCK)
            real, imag = mass[0, p, span, :], mass[1, p, span, :]
            scale = weight * inverse[p, span, :]
            images, centers = [], []
            for i in (0, 1):
                x, y, z = (field[before, p, 2 * c + i, at(r), :] for c in range(3))
                y_up = field[before, p + 1, 2 + i, at(r), :]
                z_up = field[before, p + 1, 4 + i, at(r), :]
                curl_x = mixed[before, p + 1, 4 + i, at(r), :]
                curl_y = mixed[before, p + 1, i, at(r), :] - z_up
                curl_z = y_up - mixed[before, p + 1, 2 + i, at(r), :]
                curl_x_left = mixed[before, p + 1, 4 + i, at(r - 1), :]
                curl_z_left = field[before, p + 1, 2 + i, at(r - 1), :] - mixed[before, p + 1, 2 + i, at(r - 1), :]
                curl_y_low = (mixed[before, p, i, at(r), :] - z) * inside
                curl_z_low = (y - mixed[before, p, 2 + i, at(r), :]) * inside
                images.append((
                    (behind(curl_y) - curl_y) - (curl_z_left - curl_z),
                    (curl_z_low - curl_z) - (behind(curl_x) - curl_x),
                    (curl_x_left - curl_x) - (curl_y_low - curl_y),
                ))
                centers.append((x, y, z))
            for c in range(3):
                e_r, e_i = centers[0][c], centers[1][c]
                res_r = source[c, p, span, :] - (images[0][c] + real * e_r - imag * e_i)
                res_i = source[c + 3, p, span, :] - (images[1][c] + real * e_i + imag * e_r)
                field[k, p, 2 * c, at(r), :] = e_r + scale * res_r
                field[k, p, 2 * c + 1, at(r), :] = e_i + scale * res_i

    def moments(p):
        for r in blocks:
            span = pl.ds(r, BLOCK)
            m = []
            for c in range(3):
                f_r = saved[c, p, span, :].astype(jnp.float32)
                f_i = saved[c + 3, p, span, :].astype(jnp.float32)
                a_r = field[SWEEPS - 1, p, 2 * c, at(r), :]
                a_i = field[SWEEPS - 1, p, 2 * c + 1, at(r), :]
                m.append(0.25 * (f_r * a_i + f_i * a_r))
            part[0, at(r), :] = m[0] + ahead(m[0])
            part[1, at(r), :] = m[2]
            lower[p, span, :] = m[1] + ahead(m[1])
        for r in blocks:
            span = pl.ds(r, BLOCK)
            shared = lower[p, span, :] + (part[1, at(r), :] + part[1, at(r + 1), :])
            lower[p, span, :] = shared
            upper[p, span, :] = shared + (part[0, at(r), :] + part[0, at(r + 1), :])

    def outer(t, carry):
        begin(jnp.where(t == core, 0, planes - 1))
        return carry

    lax.fori_loop(0, 2, outer, 0)
    pl.semaphore_wait(barrier, awaited)

    @pl.when(has_below)
    def _():
        halo_down(0).start()

    @pl.when(has_above)
    def _():
        halo_up(0).start()

    def inner(p, carry):
        begin(p)
        return carry

    lax.fori_loop(1, planes - 1, inner, 0)

    load_depth.wait()
    load_map.wait()
    edge_out[...] = jnp.zeros_like(edge_out)
    edge_out[0:1, 0:rows] = depth[planes - 1:planes, :].astype(jnp.float32)
    edge_out[1:2, 0:rows] = plane_map[planes - 1:planes, :].astype(jnp.float32)

    @pl.when(has_above)
    def _():
        edge_up.start()

    diagonal = lax.broadcasted_iota(jnp.int32, (rows, rows), 0) == lax.broadcasted_iota(jnp.int32, (rows, rows), 1)

    def columns(row):
        spread = jnp.where(diagonal, jnp.broadcast_to(row, (rows, rows)), 0.0)
        return jnp.broadcast_to(jnp.sum(spread, axis=1, keepdims=True), (rows, cells))

    for p in range(planes):
        how_deep[p] = columns(depth[p:p + 1, :].astype(jnp.float32))
        where_to[p] = columns(plane_map[p:p + 1, :].astype(jnp.float32))

    def turn(n, carry):
        k = n // planes + 1
        t = lax.rem(n, planes)
        outermost = t >= planes - 2
        p = jnp.where(outermost, jnp.where((t == planes - 2) == (core == 0), planes - 1, 0), t + 1)
        weight = jnp.where(k == 1, STEPS[1], jnp.where(k == 2, STEPS[2], STEPS[3])).astype(jnp.float32)

        @pl.when((p == 0) & has_below)
        def _():
            halo_up(k - 1).wait_recv()

        @pl.when((p == planes - 1) & has_above)
        def _():
            halo_down(k - 1).wait_recv()

        update(k, p, weight)

        @pl.when(k < SWEEPS - 1)
        def _():
            @pl.when((p == 0) & has_below)
            def _():
                halo_down(k).start()

            combine(k, p)

            @pl.when((p == planes - 1) & has_above)
            def _():
                halo_up(k).start()

        @pl.when(k == SWEEPS - 1)
        def _():
            @pl.when(t == 0)
            def _():
                load_saved.wait()

            moments(p)

        return carry

    lax.fori_loop(0, (SWEEPS - 1) * planes, turn, 0)

    @pl.when(has_above)
    def _():
        edge_up.wait_send()

    @pl.when(has_below)
    def _():
        edge_up.wait_recv()

    how_deep[planes] = columns(edge_in[0:1, 0:rows])
    where_to[planes] = columns(edge_in[1:2, 0:rows])

    place = lane.astype(jnp.float32)
    origin = me.astype(jnp.float32)
    for r in blocks:
        span = pl.ds(r, BLOCK)
        kept, targets = [], []
        for p in range(planes + 1):
            if p == planes:
                value = lower[0, span, :]
            elif p == planes - 1:
                value = upper[p, span, :]
            else:
                value = upper[p, span, :] + lower[p + 1, span, :]
            kept.append(jnp.where(place < how_deep[p, span, :], value, 0.0))
            targets.append(where_to[p, span, :] - origin)
        for offset in range(LOW, HIGH + 1):
            sum_here = jnp.zeros((BLOCK, cells), jnp.float32)
            for p in range(planes + 1):
                if (p == planes and offset < HIGH) or (p < planes and offset > LOW):
                    sum_here = sum_here + jnp.where(targets[p] == float(offset), kept[p], 0.0)
            window[offset - LOW, span, :] = sum_here

    halves = rows // 2
    sizes = range(HIGH - LOW + 1)
    def window_copy(slot):
        return pltpu.make_async_remote_copy(
            src_ref=sent.at[slot],
            dst_ref=landed.at[slot],
            send_sem=window_send.at[slot],
            recv_sem=window_recv.at[slot],
            device_id={"space": me + (slot + LOW)},
            device_id_type=MESH,
        )

    for slot in sizes:
        folded = window[slot, pl.ds(0, halves, stride=2), :] + window[slot, pl.ds(1, halves, stride=2), :]
        if slot + LOW == 0:
            total[...] = folded
        else:
            sent[slot] = folded

            @pl.when(present(slot + LOW))
            def _():
                window_copy(slot).start()

    for slot in sizes:
        if slot + LOW != 0:
            @pl.when(present(-(slot + LOW)))
            def _():
                window_copy(slot).wait_recv()
                total[...] += landed[slot]

    shares[group] = total[...]
    def share_copy(offset):
        return pltpu.make_async_remote_copy(
            src_ref=shares.at[group],
            dst_ref=shares.at[group],
            send_sem=share_send.at[offset - 1],
            recv_sem=share_recv.at[offset - 1],
            device_id={"src": lax.rem(group + offset, groups)},
            device_id_type=MESH,
        )

    def share_from(offset):
        slot = lax.rem(group + groups - offset, groups)
        return pltpu.make_async_remote_copy(
            src_ref=shares.at[slot],
            dst_ref=shares.at[slot],
            send_sem=share_send.at[offset - 1],
            recv_sem=share_recv.at[offset - 1],
            device_id={"src": lax.rem(group + offset, groups)},
            device_id_type=MESH,
        )

    for offset in range(1, groups):
        share_copy(offset).start()
    load_rough.wait()
    for offset in range(1, groups):
        share_from(offset).wait_recv()
    whole = shares[0]
    for slot in range(1, groups):
        whole = whole + shares[slot]

    lanes = lax.broadcasted_iota(jnp.int32, (halves, cells), 1)
    for a in range(3):
        left, middle, right = (rough[3 * a + b] * whole for b in range(3))
        row_sum = middle
        row_sum = row_sum + jnp.where(lanes == cells - 1, 0.0, pltpu.roll(left, cells - 1, 1))
        row_sum = row_sum + jnp.where(lanes == 0, 0.0, pltpu.roll(right, 1, 1))
        padded[a, pl.ds(PAD, halves), :] = row_sum
    out_ref[0] = (
        padded[1, pl.ds(PAD, halves), :]
        + padded[0, pl.ds(PAD + 1, halves), :]
        + padded[2, pl.ds(PAD - 1, halves), :]
    )

    for k in range(SWEEPS - 1):
        @pl.when(has_below)
        def _():
            halo_down(k).wait_send()

        @pl.when(has_above)
        def _():
            halo_up(k).wait_send()
    for slot in sizes:
        if slot + LOW != 0:
            @pl.when(present(slot + LOW))
            def _():
                window_copy(slot).wait_send()
    for offset in range(1, groups):
        share_copy(offset).wait_send()


def solution(mesh):
    groups, count = mesh.shape["src"], mesh.shape["space"]

    def step(adjoint_source, forward_field, medium, plane_map, depth, rough):
        parts, planes, rows, cells = adjoint_source.shape[1:]
        halves = rows // 2
        tall = rows + 2 * PAD
        slots = HIGH - LOW + 1
        f32 = jnp.float32
        dma = pltpu.SemaphoreType.DMA
        return pl.pallas_call(
            functools.partial(kernel, groups, count),
            out_shape=jax.ShapeDtypeStruct((1, halves, cells), f32),
            in_specs=[pl.BlockSpec(memory_space=pl.ANY)] * 6,
            out_specs=pl.BlockSpec(memory_space=pltpu.VMEM),
            scratch_shapes=[
                pltpu.VMEM((parts, planes, rows, cells), f32),
                pltpu.VMEM((parts, planes, rows, cells), jnp.bfloat16),
                pltpu.VMEM((2, planes, rows, cells), f32),
                pltpu.VMEM((planes, rows), jnp.int32),
                pltpu.VMEM((planes, rows), jnp.int32),
                pltpu.VMEM((9, halves, cells), f32),
                pltpu.VMEM((planes, rows, cells), f32),
                pltpu.VMEM((SWEEPS, planes + 1, 6, tall, cells), f32),
                pltpu.VMEM((SWEEPS - 1, planes + 1, 6, tall, cells), f32),
                pltpu.VMEM((2, tall, cells), f32),
                pltpu.VMEM((planes, rows, cells), f32),
                pltpu.VMEM((planes, rows, cells), f32),
                pltpu.VMEM((planes + 1, rows, cells), f32),
                pltpu.VMEM((planes + 1, rows, cells), f32),
                pltpu.VMEM((8, 128), f32),
                pltpu.VMEM((8, 128), f32),
                pltpu.VMEM((slots, rows, cells), f32),
                pltpu.VMEM((slots, halves, cells), f32),
                pltpu.VMEM((slots, halves, cells), f32),
                pltpu.VMEM((halves, cells), f32),
                pltpu.VMEM((groups, halves, cells), f32),
                pltpu.VMEM((3, halves + 2 * PAD, cells), f32),
                dma((planes,)),
                dma((planes,)),
                dma((4,)),
                dma((SWEEPS - 1, 2)),
                dma((SWEEPS - 1, 2)),
                dma((2,)),
                dma((slots,)),
                dma((slots,)),
                dma((groups - 1,)),
                dma((groups - 1,)),
            ],
            compiler_params=pltpu.CompilerParams(
                collective_id=0, has_side_effects=True, vmem_limit_bytes=62 * 1024 * 1024
            ),
            name="gradient",
        )(adjoint_source, forward_field, medium, plane_map, depth, rough)

    in_specs = (
        P("src", None, "space", None, None),
        P("src", None, "space", None, None),
        P(None, "space", None, None),
        P("space", None),
        P("src", "space", None),
        P(None, "space", None, None),
    )
    out_specs = P("space", None, None)
    return jax.shard_map(step, mesh=mesh, in_specs=in_specs, out_specs=out_specs, check_vma=False)
```

```python
import functools

import jax
import jax.numpy as jnp
from jax import lax
from jax.experimental import pallas as pl
from jax.experimental.pallas import tpu as pltpu
from jax.sharding import PartitionSpec as P

MESH = pl.DeviceIdType.MESH
SWEEPS = 4
REACH = 2
STEPS = (0.323, 1.658, 0.422, 0.752)
PAD = 8
BLOCK = 16
PIECES = 4
LOW, HIGH = -REACH - 1, REACH


def kernel(
    groups, count,
    source_hbm, saved_hbm, medium_hbm, map_hbm, depth_hbm, rough_hbm,
    out_ref,
    source, saved, mass, plane_map, depth, rough,
    inverse, field, mixed, part, upper, lower, where_to, how_deep, edge_out, edge_in,
    window, sent, landed, total, shares, padded,
    source_sem, mass_sem, load_sem, halo_send, halo_recv, edge_sem, window_send, window_recv, share_send, share_recv,
):
    planes, rows, cells = source.shape[1:]
    group = lax.axis_index("src")
    me = lax.axis_index("space")
    core = lax.rem(me, 2)
    has_below, has_above = me > 0, me < count - 1
    blocks = range(0, rows, BLOCK)
    lane = lax.broadcasted_iota(jnp.int32, (BLOCK, cells), 1)
    first_lane, last_lane = lane == 0, lane == cells - 1

    def at(start):
        return pl.ds(PAD + start, BLOCK)

    def ahead(value):
        return jnp.where(last_lane, 0.0, pltpu.roll(value, cells - 1, 1))

    def behind(value):
        return jnp.where(first_lane, 0.0, pltpu.roll(value, 1, 1))

    def present(offset):
        other = me + offset
        return (other >= 0) & (other < count)

    barrier = pltpu.get_barrier_semaphore()
    awaited = groups - 1
    for offset in (1, -1, 2, -2, 3):
        @pl.when(present(offset))
        def _():
            pl.semaphore_signal(barrier, inc=1, device_id={"space": me + offset}, device_id_type=MESH)
    for offset in range(1, groups):
        pl.semaphore_signal(barrier, inc=1, device_id={"src": lax.rem(group + offset, groups)}, device_id_type=MESH)
    for offset in range(LOW, HIGH + 1):
        if offset != 0:
            awaited = awaited + present(offset).astype(jnp.int32)

    def load_source(p):
        return pltpu.make_async_copy(source_hbm.at[0, :, p], source.at[:, p], source_sem.at[p])

    def load_mass(p):
        return pltpu.make_async_copy(medium_hbm.at[:, p], mass.at[:, p], mass_sem.at[p])

    for p in (0, planes - 1, *range(1, planes - 1)):
        load_source(p).start()
        load_mass(p).start()
    load_depth = pltpu.make_async_copy(depth_hbm.at[0], depth, load_sem.at[0])
    load_map = pltpu.make_async_copy(map_hbm, plane_map, load_sem.at[1])
    load_saved = pltpu.make_async_copy(saved_hbm.at[0], saved, load_sem.at[2])
    load_rough = pltpu.make_async_copy(rough_hbm.at[:, 0], rough, load_sem.at[3])
    for load in (load_depth, load_map, load_saved, load_rough):
        load.start()

    margin = jnp.zeros((PAD, cells), jnp.float32)
    for k in range(SWEEPS - 1):
        for p in range(planes):
            for c in (0, 1, 4, 5):
                field[k, p, c, pl.ds(PAD + rows, PAD), :] = margin
            for c in (2, 3):
                field[k, p + 1, c, pl.ds(0, PAD), :] = margin
                mixed[k, p + 1, c, pl.ds(0, PAD), :] = margin
            for c in (4, 5):
                mixed[k, p + 1, c, pl.ds(0, PAD), :] = margin
    for p in range(planes):
        for c in (0, 1):
            part[p, c, pl.ds(PAD + rows, PAD), :] = margin
    padded[...] = jnp.zeros_like(padded)

    @pl.when(jnp.logical_not(has_below))
    def _():
        for k in range(SWEEPS - 1):
            mixed[k, 0] = jnp.zeros(mixed.shape[2:], jnp.float32)
        edge_in[...] = jnp.full(edge_in.shape, -1000.0, jnp.float32)

    @pl.when(jnp.logical_not(has_above))
    def _():
        for k in range(SWEEPS - 1):
            field[k, planes, 2:6] = jnp.zeros((4, *field.shape[3:]), jnp.float32)

    piece = rows // PIECES

    def rows_of(q):
        return pl.ds(PAD + q * piece, piece)

    def halo_down(k, q):
        return pltpu.make_async_remote_copy(
            src_ref=field.at[k, 0, 2:6, rows_of(q)],
            dst_ref=field.at[k, planes, 2:6, rows_of(q)],
            send_sem=halo_send.at[k, 0, q],
            recv_sem=halo_recv.at[k, 0, q],
            device_id={"space": me - 1},
            device_id_type=MESH,
        )

    def halo_up(k, q):
        return pltpu.make_async_remote_copy(
            src_ref=mixed.at[k, planes, 0:4, rows_of(q)],
            dst_ref=mixed.at[k, 0, 0:4, rows_of(q)],
            send_sem=halo_send.at[k, 1, q],
            recv_sem=halo_recv.at[k, 1, q],
            device_id={"space": me + 1},
            device_id_type=MESH,
        )

    edge_up = pltpu.make_async_remote_copy(
        src_ref=edge_out,
        dst_ref=edge_in,
        send_sem=edge_sem.at[0],
        recv_sem=edge_sem.at[1],
        device_id={"space": me + 1},
        device_id_type=MESH,
    )

    def combine(k, p, span=blocks):
        for r in span:
            for i in (0, 1):
                x, y, z = (field[k, p, 2 * c + i, at(r), :] for c in range(3))
                x_next, z_next = (field[k, p, 2 * c + i, at(r + 1), :] for c in (0, 2))
                mixed[k, p + 1, i, at(r), :] = (ahead(x) - x) + z
                mixed[k, p + 1, 2 + i, at(r), :] = y + (x_next - x)
                mixed[k, p + 1, 4 + i, at(r), :] = (z_next - z) - (ahead(y) - y)

    def begin(p):
        load_source(p).wait()
        load_mass(p).wait()
        for r in blocks:
            span = pl.ds(r, BLOCK)
            turned = 1.0 / (4.0 + mass[0, p, span, :])
            inverse[p, span, :] = turned
            turned = STEPS[0] * turned
            for c in range(3):
                for i in (0, 1):
                    field[0, p, 2 * c + i, at(r), :] = source[c + 3 * i, p, span, :] * turned
        combine(0, p)

    def update(k, p, weight, span_of=blocks):
        before = k - 1
        inside = jnp.where((me == 0) & (p == 0), 0.0, 1.0).astype(jnp.float32)
        for r in span_of:
            span = pl.ds(r, BLOCK)
            real, imag = mass[0, p, span, :], mass[1, p, span, :]
            scale = weight * inverse[p, span, :]
            images, centers = [], []
            for i in (0, 1):
                x, y, z = (field[before, p, 2 * c + i, at(r), :] for c in range(3))
                y_up = field[before, p + 1, 2 + i, at(r), :]
                z_up = field[before, p + 1, 4 + i, at(r), :]
                curl_x = mixed[before, p + 1, 4 + i, at(r), :]
                curl_y = mixed[before, p + 1, i, at(r), :] - z_up
                curl_z = y_up - mixed[before, p + 1, 2 + i, at(r), :]
                curl_x_left = mixed[before, p + 1, 4 + i, at(r - 1), :]
                curl_z_left = field[before, p + 1, 2 + i, at(r - 1), :] - mixed[before, p + 1, 2 + i, at(r - 1), :]
                curl_y_low = (mixed[before, p, i, at(r), :] - z) * inside
                curl_z_low = (y - mixed[before, p, 2 + i, at(r), :]) * inside
                images.append((
                    (behind(curl_y) - curl_y) - (curl_z_left - curl_z),
                    (curl_z_low - curl_z) - (behind(curl_x) - curl_x),
                    (curl_x_left - curl_x) - (curl_y_low - curl_y),
                ))
                centers.append((x, y, z))
            for c in range(3):
                e_r, e_i = centers[0][c], centers[1][c]
                res_r = source[c, p, span, :] - (images[0][c] + real * e_r - imag * e_i)
                res_i = source[c + 3, p, span, :] - (images[1][c] + real * e_i + imag * e_r)
                field[k, p, 2 * c, at(r), :] = e_r + scale * res_r
                field[k, p, 2 * c + 1, at(r), :] = e_i + scale * res_i

    def products(p, span_of=blocks):
        for r in span_of:
            span = pl.ds(r, BLOCK)
            m = []
            for c in range(3):
                f_r = saved[c, p, span, :].astype(jnp.float32)
                f_i = saved[c + 3, p, span, :].astype(jnp.float32)
                a_r = field[SWEEPS - 1, p, 2 * c, at(r), :]
                a_i = field[SWEEPS - 1, p, 2 * c + 1, at(r), :]
                m.append(0.25 * (f_r * a_i + f_i * a_r))
            part[p, 0, at(r), :] = m[0] + ahead(m[0])
            part[p, 1, at(r), :] = m[2]
            lower[p, span, :] = m[1] + ahead(m[1])

    def averages(p, span_of=blocks):
        for r in span_of:
            span = pl.ds(r, BLOCK)
            shared = lower[p, span, :] + (part[p, 1, at(r), :] + part[p, 1, at(r + 1), :])
            lower[p, span, :] = shared
            upper[p, span, :] = shared + (part[p, 0, at(r), :] + part[p, 0, at(r + 1), :])

    place = lane.astype(jnp.float32)
    origin = me.astype(jnp.float32)
    halves = rows // 2
    slots = range(HIGH - LOW + 1)

    def window_sums(r):
        span = pl.ds(r, BLOCK)
        kept, targets = [], []
        for p in range(planes + 1):
            if p == planes:
                value = lower[0, span, :]
            elif p == planes - 1:
                value = upper[p, span, :]
            else:
                value = upper[p, span, :] + lower[p + 1, span, :]
            kept.append(jnp.where(place < how_deep[p, span, :], value, 0.0))
            targets.append(where_to[p, span, :] - origin)
        for slot in slots:
            offset = slot + LOW
            terms = [p for p in range(planes + 1) if (p == planes and offset < HIGH) or (p < planes and offset > LOW)]
            sum_here = jnp.zeros((BLOCK, cells), jnp.float32)
            for p in terms:
                sum_here = sum_here + jnp.where(targets[p] == float(offset), kept[p], 0.0)
            window[slot, span, :] = sum_here
            folded = window[slot, pl.ds(r, BLOCK // 2, stride=2), :] + window[slot, pl.ds(r + 1, BLOCK // 2, stride=2), :]
            sent[slot, pl.ds(r // 2, BLOCK // 2), :] = folded

    def outer(t, carry):
        begin(jnp.where(t == core, 0, planes - 1))
        return carry

    lax.fori_loop(0, 2, outer, 0)
    pl.semaphore_wait(barrier, awaited)

    @pl.when(has_below)
    def _():
        for q in range(PIECES):
            halo_down(0, q).start()

    @pl.when(has_above)
    def _():
        for q in range(PIECES):
            halo_up(0, q).start()

    def inner(p, carry):
        begin(p)
        return carry

    lax.fori_loop(1, planes - 1, inner, 0)

    load_depth.wait()
    load_map.wait()
    edge_out[...] = jnp.zeros_like(edge_out)
    edge_out[0:1, 0:rows] = depth[planes - 1:planes, :].astype(jnp.float32)
    edge_out[1:2, 0:rows] = plane_map[planes - 1:planes, :].astype(jnp.float32)

    @pl.when(has_above)
    def _():
        edge_up.start()

    diagonal = lax.broadcasted_iota(jnp.int32, (rows, rows), 0) == lax.broadcasted_iota(jnp.int32, (rows, rows), 1)

    def columns(row):
        spread = jnp.where(diagonal, jnp.broadcast_to(row, (rows, rows)), 0.0)
        return jnp.broadcast_to(jnp.sum(spread, axis=1, keepdims=True), (rows, cells))

    for p in range(planes):
        how_deep[p] = columns(depth[p:p + 1, :].astype(jnp.float32))
        where_to[p] = columns(plane_map[p:p + 1, :].astype(jnp.float32))

    def await_halo(k, p, q):
        @pl.when((p == 0) & has_below)
        def _():
            halo_up(k, q).wait_recv()

        @pl.when((p == planes - 1) & has_above)
        def _():
            halo_down(k, q).wait_recv()

    def blocks_of(q):
        return range(q * piece, (q + 1) * piece, BLOCK)

    def end_at(t):
        return jnp.where(t == core, planes - 1, 0)

    def complete_after(q):
        return [q - 1] * (q > 0) + [q] * (q == PIECES - 1)

    def turn(k, carry):
        weight = jnp.where(k == 1, STEPS[1], STEPS[2]).astype(jnp.float32)

        def middle(p, carry):
            update(k, p, weight)
            combine(k, p)
            return carry

        lax.fori_loop(1, planes - 1, middle, 0)

        for q in range(PIECES):
            def ends(t, carry):
                p = end_at(t)
                await_halo(k - 1, p, q)
                update(k, p, weight, blocks_of(q))

                @pl.when((p == 0) & has_below)
                def _():
                    halo_down(k, q).start()

                for ready in complete_after(q):
                    combine(k, p, blocks_of(ready))

                    @pl.when((p == planes - 1) & has_above)
                    def _():
                        halo_up(k, ready).start()

                return carry

            lax.fori_loop(0, 2, ends, 0)
        return carry

    lax.fori_loop(1, SWEEPS - 1, turn, 0)

    last = SWEEPS - 1
    load_saved.wait()

    def middle(p, carry):
        update(last, p, STEPS[last])
        products(p)
        averages(p)
        return carry

    lax.fori_loop(1, planes - 1, middle, 0)

    @pl.when(has_above)
    def _():
        edge_up.wait_send()

    @pl.when(has_below)
    def _():
        edge_up.wait_recv()

    how_deep[planes] = columns(edge_in[0:1, 0:rows])
    where_to[planes] = columns(edge_in[1:2, 0:rows])

    for q in range(PIECES):
        def ends(t, carry):
            p = end_at(t)
            await_halo(last - 1, p, q)
            update(last, p, STEPS[last], blocks_of(q))
            products(p, blocks_of(q))
            for ready in complete_after(q):
                averages(p, blocks_of(ready))
            return carry

        lax.fori_loop(0, 2, ends, 0)
        for ready in complete_after(q):
            for r in blocks_of(ready):
                window_sums(r)

    def window_copy(slot):
        return pltpu.make_async_remote_copy(
            src_ref=sent.at[slot],
            dst_ref=landed.at[slot],
            send_sem=window_send.at[slot],
            recv_sem=window_recv.at[slot],
            device_id={"space": me + (slot + LOW)},
            device_id_type=MESH,
        )

    for slot in sorted(slots, key=lambda slot: -abs(slot + LOW)):
        if slot + LOW != 0:
            @pl.when(present(slot + LOW))
            def _():
                window_copy(slot).start()

    total[...] = sent[-LOW]
    for slot in slots:
        if slot + LOW != 0:
            @pl.when(present(-(slot + LOW)))
            def _():
                window_copy(slot).wait_recv()
                total[...] += landed[slot]

    shares[group] = total[...]
    def share_copy(offset):
        return pltpu.make_async_remote_copy(
            src_ref=shares.at[group],
            dst_ref=shares.at[group],
            send_sem=share_send.at[offset - 1],
            recv_sem=share_recv.at[offset - 1],
            device_id={"src": lax.rem(group + offset, groups)},
            device_id_type=MESH,
        )

    def share_from(offset):
        slot = lax.rem(group + groups - offset, groups)
        return pltpu.make_async_remote_copy(
            src_ref=shares.at[slot],
            dst_ref=shares.at[slot],
            send_sem=share_send.at[offset - 1],
            recv_sem=share_recv.at[offset - 1],
            device_id={"src": lax.rem(group + offset, groups)},
            device_id_type=MESH,
        )

    for offset in sorted(range(1, groups), key=lambda offset: -min(offset, groups - offset)):
        share_copy(offset).start()

    for k in range(SWEEPS - 1):
        @pl.when(has_below)
        def _():
            for q in range(PIECES):
                halo_down(k, q).wait_send()

        @pl.when(has_above)
        def _():
            for q in range(PIECES):
                halo_up(k, q).wait_send()
    for slot in slots:
        if slot + LOW != 0:
            @pl.when(present(slot + LOW))
            def _():
                window_copy(slot).wait_send()
    load_rough.wait()
    for offset in range(1, groups):
        share_from(offset).wait_recv()
    whole = shares[0]
    for slot in range(1, groups):
        whole = whole + shares[slot]

    lanes = lax.broadcasted_iota(jnp.int32, (halves, cells), 1)
    for a in range(3):
        left, middle, right = (rough[3 * a + b] * whole for b in range(3))
        row_sum = middle
        row_sum = row_sum + jnp.where(lanes == cells - 1, 0.0, pltpu.roll(left, cells - 1, 1))
        row_sum = row_sum + jnp.where(lanes == 0, 0.0, pltpu.roll(right, 1, 1))
        padded[a, pl.ds(PAD, halves), :] = row_sum
    out_ref[0] = (
        padded[1, pl.ds(PAD, halves), :]
        + padded[0, pl.ds(PAD + 1, halves), :]
        + padded[2, pl.ds(PAD - 1, halves), :]
    )

    for offset in range(1, groups):
        share_copy(offset).wait_send()


def solution(mesh):
    groups, count = mesh.shape["src"], mesh.shape["space"]

    def step(adjoint_source, forward_field, medium, plane_map, depth, rough):
        parts, planes, rows, cells = adjoint_source.shape[1:]
        halves = rows // 2
        tall = rows + 2 * PAD
        slots = HIGH - LOW + 1
        f32 = jnp.float32
        dma = pltpu.SemaphoreType.DMA
        return pl.pallas_call(
            functools.partial(kernel, groups, count),
            out_shape=jax.ShapeDtypeStruct((1, halves, cells), f32),
            in_specs=[pl.BlockSpec(memory_space=pltpu.HBM)] * 6,
            out_specs=pl.BlockSpec(memory_space=pltpu.VMEM),
            scratch_shapes=[
                pltpu.VMEM((parts, planes, rows, cells), f32),
                pltpu.VMEM((parts, planes, rows, cells), jnp.bfloat16),
                pltpu.VMEM((2, planes, rows, cells), f32),
                pltpu.VMEM((planes, rows), jnp.int32),
                pltpu.VMEM((planes, rows), jnp.int32),
                pltpu.VMEM((9, halves, cells), f32),
                pltpu.VMEM((planes, rows, cells), f32),
                pltpu.VMEM((SWEEPS, planes + 1, 6, tall, cells), f32),
                pltpu.VMEM((SWEEPS - 1, planes + 1, 6, tall, cells), f32),
                pltpu.VMEM((planes, 2, tall, cells), f32),
                pltpu.VMEM((planes, rows, cells), f32),
                pltpu.VMEM((planes, rows, cells), f32),
                pltpu.VMEM((planes + 1, rows, cells), f32),
                pltpu.VMEM((planes + 1, rows, cells), f32),
                pltpu.VMEM((8, 128), f32),
                pltpu.VMEM((8, 128), f32),
                pltpu.VMEM((slots, rows, cells), f32),
                pltpu.VMEM((slots, halves, cells), f32),
                pltpu.VMEM((slots, halves, cells), f32),
                pltpu.VMEM((halves, cells), f32),
                pltpu.VMEM((groups, halves, cells), f32),
                pltpu.VMEM((3, halves + 2 * PAD, cells), f32),
                dma((planes,)),
                dma((planes,)),
                dma((4,)),
                dma((SWEEPS - 1, 2, PIECES)),
                dma((SWEEPS - 1, 2, PIECES)),
                dma((2,)),
                dma((slots,)),
                dma((slots,)),
                dma((groups - 1,)),
                dma((groups - 1,)),
            ],
            compiler_params=pltpu.CompilerParams(
                collective_id=0, has_side_effects=True, vmem_limit_bytes=48 * 1024 * 1024
            ),
            name="gradient",
        )(*(pltpu.with_memory_space_constraint(given, pltpu.HBM) for given in (adjoint_source, forward_field, medium, plane_map, depth, rough)))

    in_specs = (
        P("src", None, "space", None, None),
        P("src", None, "space", None, None),
        P(None, "space", None, None),
        P("space", None),
        P("src", "space", None),
        P(None, "space", None, None),
    )
    out_specs = P("space", None, None)
    return jax.shard_map(step, mesh=mesh, in_specs=in_specs, out_specs=out_specs, check_vma=False)
```

```python
import functools

import jax
import jax.numpy as jnp
from jax import lax
from jax.experimental import pallas as pl
from jax.experimental.pallas import tpu as pltpu
from jax.sharding import PartitionSpec as P

MESH = pl.DeviceIdType.MESH
SWEEPS = 4
REACH = 2
STEPS = (0.323, 1.658, 0.422, 0.752)
PAD = 8
BLOCK = 16
PIECES = 4
LOW, HIGH = -REACH - 1, REACH


def kernel(
    groups, count,
    source_hbm, saved_hbm, medium_hbm, map_hbm, depth_hbm, rough_hbm,
    out_ref,
    source, saved, mass, plane_map, depth, rough,
    inverse, field, mixed, part, upper, lower, where_to, how_deep, edge_out, edge_in,
    window, sent, landed, total, shares, padded,
    source_sem, mass_sem, load_sem, halo_send, halo_recv, edge_sem, window_send, window_recv, share_send, share_recv,
):
    planes, rows, cells = source.shape[1:]
    group = lax.axis_index("src")
    me = lax.axis_index("space")
    core = lax.rem(me, 2)
    has_below, has_above = me > 0, me < count - 1
    blocks = range(0, rows, BLOCK)
    lane = lax.broadcasted_iota(jnp.int32, (BLOCK, cells), 1)
    first_lane, last_lane = lane == 0, lane == cells - 1

    def at(start):
        return pl.ds(PAD + start, BLOCK)

    def ahead(value):
        return jnp.where(last_lane, 0.0, pltpu.roll(value, cells - 1, 1))

    def behind(value):
        return jnp.where(first_lane, 0.0, pltpu.roll(value, 1, 1))

    def present(offset):
        other = me + offset
        return (other >= 0) & (other < count)

    across = 1 - 2 * core
    even = core == 0

    barrier = pltpu.get_barrier_semaphore()
    for low, high in ((1, 1), (-1, -1), (2, 2), (3, -2), (4, -3)):
        offset = jnp.where(even, low, high)

        @pl.when(present(offset))
        def _():
            pl.semaphore_signal(barrier, inc=1, device_id={"space": me + offset}, device_id_type=MESH)
    for offset in range(1, groups):
        pl.semaphore_signal(
            barrier, inc=1,
            device_id={"src": lax.rem(group + offset, groups), "space": me + across},
            device_id_type=MESH,
        )
    awaited = groups - 1
    for low, high in ((1, 1), (-1, -1), (-2, -2), (-4, 2), (3, -3)):
        awaited = awaited + present(jnp.where(even, low, high)).astype(jnp.int32)

    def load_source(p):
        return pltpu.make_async_copy(source_hbm.at[0, :, p], source.at[:, p], source_sem.at[p])

    def load_mass(p):
        return pltpu.make_async_copy(medium_hbm.at[:, p], mass.at[:, p], mass_sem.at[p])

    for p in (0, planes - 1, *range(1, planes - 1)):
        load_source(p).start()
        load_mass(p).start()
    load_depth = pltpu.make_async_copy(depth_hbm.at[0], depth, load_sem.at[0])
    load_map = pltpu.make_async_copy(map_hbm, plane_map, load_sem.at[1])
    load_saved = pltpu.make_async_copy(saved_hbm.at[0], saved, load_sem.at[2])
    load_rough = pltpu.make_async_copy(rough_hbm.at[:, 0], rough, load_sem.at[3])
    for load in (load_depth, load_map, load_saved, load_rough):
        load.start()

    margin = jnp.zeros((PAD, cells), jnp.float32)
    for k in range(SWEEPS - 1):
        for p in range(planes):
            for c in (0, 1, 4, 5):
                field[k, p, c, pl.ds(PAD + rows, PAD), :] = margin
            for c in (2, 3):
                field[k, p + 1, c, pl.ds(0, PAD), :] = margin
                mixed[k, p + 1, c, pl.ds(0, PAD), :] = margin
            for c in (4, 5):
                mixed[k, p + 1, c, pl.ds(0, PAD), :] = margin
    for p in range(planes):
        for c in (0, 1):
            part[p, c, pl.ds(PAD + rows, PAD), :] = margin
    padded[...] = jnp.zeros_like(padded)

    @pl.when(jnp.logical_not(has_below))
    def _():
        for k in range(SWEEPS - 1):
            mixed[k, 0] = jnp.zeros(mixed.shape[2:], jnp.float32)
        edge_in[...] = jnp.full(edge_in.shape, -1000.0, jnp.float32)

    @pl.when(jnp.logical_not(has_above))
    def _():
        for k in range(SWEEPS - 1):
            field[k, planes, 2:6] = jnp.zeros((4, *field.shape[3:]), jnp.float32)

    piece = rows // PIECES

    def rows_of(q):
        return pl.ds(PAD + q * piece, piece)

    def halo_down(k, q):
        return pltpu.make_async_remote_copy(
            src_ref=field.at[k, 0, 2:6, rows_of(q)],
            dst_ref=field.at[k, planes, 2:6, rows_of(q)],
            send_sem=halo_send.at[k, 0, q],
            recv_sem=halo_recv.at[k, 0, q],
            device_id={"space": me - 1},
            device_id_type=MESH,
        )

    def halo_up(k, q):
        return pltpu.make_async_remote_copy(
            src_ref=mixed.at[k, planes, 0:4, rows_of(q)],
            dst_ref=mixed.at[k, 0, 0:4, rows_of(q)],
            send_sem=halo_send.at[k, 1, q],
            recv_sem=halo_recv.at[k, 1, q],
            device_id={"space": me + 1},
            device_id_type=MESH,
        )

    edge_up = pltpu.make_async_remote_copy(
        src_ref=edge_out,
        dst_ref=edge_in,
        send_sem=edge_sem.at[0],
        recv_sem=edge_sem.at[1],
        device_id={"space": me + 1},
        device_id_type=MESH,
    )

    def combine(k, p, span=blocks):
        for r in span:
            for i in (0, 1):
                x, y, z = (field[k, p, 2 * c + i, at(r), :] for c in range(3))
                x_next, z_next = (field[k, p, 2 * c + i, at(r + 1), :] for c in (0, 2))
                mixed[k, p + 1, i, at(r), :] = (ahead(x) - x) + z
                mixed[k, p + 1, 2 + i, at(r), :] = y + (x_next - x)
                mixed[k, p + 1, 4 + i, at(r), :] = (z_next - z) - (ahead(y) - y)

    def begin(p):
        load_source(p).wait()
        load_mass(p).wait()
        for r in blocks:
            span = pl.ds(r, BLOCK)
            turned = 1.0 / (4.0 + mass[0, p, span, :])
            inverse[p, span, :] = turned
            turned = STEPS[0] * turned
            for c in range(3):
                for i in (0, 1):
                    field[0, p, 2 * c + i, at(r), :] = source[c + 3 * i, p, span, :] * turned
        combine(0, p)

    def update(k, p, weight, span_of=blocks):
        before = k - 1
        inside = jnp.where((me == 0) & (p == 0), 0.0, 1.0).astype(jnp.float32)
        for r in span_of:
            span = pl.ds(r, BLOCK)
            real, imag = mass[0, p, span, :], mass[1, p, span, :]
            scale = weight * inverse[p, span, :]
            images, centers = [], []
            for i in (0, 1):
                x, y, z = (field[before, p, 2 * c + i, at(r), :] for c in range(3))
                y_up = field[before, p + 1, 2 + i, at(r), :]
                z_up = field[before, p + 1, 4 + i, at(r), :]
                curl_x = mixed[before, p + 1, 4 + i, at(r), :]
                curl_y = mixed[before, p + 1, i, at(r), :] - z_up
                curl_z = y_up - mixed[before, p + 1, 2 + i, at(r), :]
                curl_x_left = mixed[before, p + 1, 4 + i, at(r - 1), :]
                curl_z_left = field[before, p + 1, 2 + i, at(r - 1), :] - mixed[before, p + 1, 2 + i, at(r - 1), :]
                curl_y_low = (mixed[before, p, i, at(r), :] - z) * inside
                curl_z_low = (y - mixed[before, p, 2 + i, at(r), :]) * inside
                images.append((
                    (behind(curl_y) - curl_y) - (curl_z_left - curl_z),
                    (curl_z_low - curl_z) - (behind(curl_x) - curl_x),
                    (curl_x_left - curl_x) - (curl_y_low - curl_y),
                ))
                centers.append((x, y, z))
            for c in range(3):
                e_r, e_i = centers[0][c], centers[1][c]
                res_r = source[c, p, span, :] - (images[0][c] + real * e_r - imag * e_i)
                res_i = source[c + 3, p, span, :] - (images[1][c] + real * e_i + imag * e_r)
                field[k, p, 2 * c, at(r), :] = e_r + scale * res_r
                field[k, p, 2 * c + 1, at(r), :] = e_i + scale * res_i

    def products(p, span_of=blocks):
        for r in span_of:
            span = pl.ds(r, BLOCK)
            m = []
            for c in range(3):
                f_r = saved[c, p, span, :].astype(jnp.float32)
                f_i = saved[c + 3, p, span, :].astype(jnp.float32)
                a_r = field[SWEEPS - 1, p, 2 * c, at(r), :]
                a_i = field[SWEEPS - 1, p, 2 * c + 1, at(r), :]
                m.append(0.25 * (f_r * a_i + f_i * a_r))
            part[p, 0, at(r), :] = m[0] + ahead(m[0])
            part[p, 1, at(r), :] = m[2]
            lower[p, span, :] = m[1] + ahead(m[1])

    def averages(p, span_of=blocks):
        for r in span_of:
            span = pl.ds(r, BLOCK)
            shared = lower[p, span, :] + (part[p, 1, at(r), :] + part[p, 1, at(r + 1), :])
            lower[p, span, :] = shared
            upper[p, span, :] = shared + (part[p, 0, at(r), :] + part[p, 0, at(r + 1), :])

    place = lane.astype(jnp.float32)
    origin = me.astype(jnp.float32)
    halves = rows // 2
    slots = range(HIGH - LOW + 1)

    def window_sums(r):
        span = pl.ds(r, BLOCK)
        kept, targets = [], []
        for p in range(planes + 1):
            if p == planes:
                value = lower[0, span, :]
            elif p == planes - 1:
                value = upper[p, span, :]
            else:
                value = upper[p, span, :] + lower[p + 1, span, :]
            kept.append(jnp.where(place < how_deep[p, span, :], value, 0.0))
            targets.append(where_to[p, span, :] - origin)
        for slot in slots:
            offset = slot + LOW
            terms = [p for p in range(planes + 1) if (p == planes and offset < HIGH) or (p < planes and offset > LOW)]
            sum_here = jnp.zeros((BLOCK, cells), jnp.float32)
            for p in terms:
                sum_here = sum_here + jnp.where(targets[p] == float(offset), kept[p], 0.0)
            window[slot, span, :] = sum_here
            folded = window[slot, pl.ds(r, BLOCK // 2, stride=2), :] + window[slot, pl.ds(r + 1, BLOCK // 2, stride=2), :]
            sent[slot, pl.ds(r // 2, BLOCK // 2), :] = folded

    def outer(t, carry):
        begin(jnp.where(t == core, 0, planes - 1))
        return carry

    lax.fori_loop(0, 2, outer, 0)
    pl.semaphore_wait(barrier, awaited)

    for q in range(PIECES):
        @pl.when(has_below)
        def _():
            halo_down(0, q).start()

        @pl.when(has_above)
        def _():
            halo_up(0, q).start()

    def inner(p, carry):
        begin(p)
        return carry

    lax.fori_loop(1, planes - 1, inner, 0)

    load_depth.wait()
    load_map.wait()
    edge_out[...] = jnp.zeros_like(edge_out)
    edge_out[0:1, 0:rows] = depth[planes - 1:planes, :].astype(jnp.float32)
    edge_out[1:2, 0:rows] = plane_map[planes - 1:planes, :].astype(jnp.float32)

    @pl.when(has_above)
    def _():
        edge_up.start()

    diagonal = lax.broadcasted_iota(jnp.int32, (rows, rows), 0) == lax.broadcasted_iota(jnp.int32, (rows, rows), 1)

    def columns(row):
        spread = jnp.where(diagonal, jnp.broadcast_to(row, (rows, rows)), 0.0)
        return jnp.broadcast_to(jnp.sum(spread, axis=1, keepdims=True), (rows, cells))

    for p in range(planes):
        how_deep[p] = columns(depth[p:p + 1, :].astype(jnp.float32))
        where_to[p] = columns(plane_map[p:p + 1, :].astype(jnp.float32))

    def await_halo(k, p, q):
        @pl.when((p == 0) & has_below)
        def _():
            halo_up(k, q).wait_recv()

        @pl.when((p == planes - 1) & has_above)
        def _():
            halo_down(k, q).wait_recv()

    def blocks_of(q):
        return range(q * piece, (q + 1) * piece, BLOCK)

    def end_at(t):
        return jnp.where(t == core, planes - 1, 0)

    def complete_after(q):
        return [q - 1] * (q > 0) + [q] * (q == PIECES - 1)

    def turn(k, carry):
        weight = jnp.where(k == 1, STEPS[1], STEPS[2]).astype(jnp.float32)

        def middle(p, carry):
            update(k, p, weight)
            combine(k, p)
            return carry

        lax.fori_loop(1, planes - 1, middle, 0)

        for q in range(PIECES):
            def ends(t, carry):
                p = end_at(t)
                await_halo(k - 1, p, q)
                update(k, p, weight, blocks_of(q))

                @pl.when((p == 0) & has_below)
                def _():
                    halo_down(k, q).start()

                for ready in complete_after(q):
                    combine(k, p, blocks_of(ready))

                    @pl.when((p == planes - 1) & has_above)
                    def _():
                        halo_up(k, ready).start()

                return carry

            lax.fori_loop(0, 2, ends, 0)
        return carry

    lax.fori_loop(1, SWEEPS - 1, turn, 0)

    last = SWEEPS - 1
    load_saved.wait()

    def middle(p, carry):
        update(last, p, STEPS[last])
        products(p)
        averages(p)
        return carry

    lax.fori_loop(1, planes - 1, middle, 0)

    @pl.when(has_above)
    def _():
        edge_up.wait_send()

    @pl.when(has_below)
    def _():
        edge_up.wait_recv()

    how_deep[planes] = columns(edge_in[0:1, 0:rows])
    where_to[planes] = columns(edge_in[1:2, 0:rows])

    for q in range(PIECES):
        def ends(t, carry):
            p = end_at(t)
            await_halo(last - 1, p, q)
            update(last, p, STEPS[last], blocks_of(q))
            products(p, blocks_of(q))
            for ready in complete_after(q):
                averages(p, blocks_of(ready))
            return carry

        lax.fori_loop(0, 2, ends, 0)
        for ready in complete_after(q):
            for r in blocks_of(ready):
                window_sums(r)

    def window_copy(slot):
        offset = slot + LOW
        return pltpu.make_async_remote_copy(
            src_ref=sent.at[slot],
            dst_ref=landed.at[slot],
            send_sem=window_send.at[slot],
            recv_sem=window_recv.at[slot],
            device_id={"space": me + offset + (across if offset % 2 == 0 else -across)},
            device_id_type=MESH,
        )

    def leaves(slot):
        offset = slot + LOW
        return present(offset) & (offset != across)

    def lands(slot):
        offset = slot + LOW
        return present(across - offset) & (offset != across)

    farthest_first = sorted(slots, key=lambda slot: -abs(slot + LOW))
    for slot in farthest_first:
        @pl.when(leaves(slot))
        def _():
            window_copy(slot).start()

    total[...] = sent[across - LOW]
    for slot in farthest_first[::-1]:
        @pl.when(lands(slot))
        def _():
            window_copy(slot).wait_recv()
            total[...] += landed[slot]

    def share_copy(offset):
        return pltpu.make_async_remote_copy(
            src_ref=total,
            dst_ref=shares.at[group],
            send_sem=share_send.at[offset],
            recv_sem=share_recv.at[offset],
            device_id={"src": lax.rem(group + offset, groups), "space": me + across},
            device_id_type=MESH,
        )

    def share_from(offset):
        return pltpu.make_async_remote_copy(
            src_ref=total,
            dst_ref=shares.at[lax.rem(group + groups - offset, groups)],
            send_sem=share_send.at[offset],
            recv_sem=share_recv.at[offset],
            device_id={"src": lax.rem(group + offset, groups), "space": me + across},
            device_id_type=MESH,
        )

    for offset in sorted(range(groups), key=lambda offset: -min(offset, groups - offset)):
        share_copy(offset).start()

    for k in range(SWEEPS - 1):
        @pl.when(has_below)
        def _():
            for q in range(PIECES):
                halo_down(k, q).wait_send()

        @pl.when(has_above)
        def _():
            for q in range(PIECES):
                halo_up(k, q).wait_send()
    for slot in slots:
        @pl.when(leaves(slot))
        def _():
            window_copy(slot).wait_send()
    load_rough.wait()
    for offset in range(groups):
        share_from(offset).wait_recv()
    whole = shares[0]
    for slot in range(1, groups):
        whole = whole + shares[slot]

    lanes = lax.broadcasted_iota(jnp.int32, (halves, cells), 1)
    for a in range(3):
        left, middle, right = (rough[3 * a + b] * whole for b in range(3))
        row_sum = middle
        row_sum = row_sum + jnp.where(lanes == cells - 1, 0.0, pltpu.roll(left, cells - 1, 1))
        row_sum = row_sum + jnp.where(lanes == 0, 0.0, pltpu.roll(right, 1, 1))
        padded[a, pl.ds(PAD, halves), :] = row_sum
    out_ref[0] = (
        padded[1, pl.ds(PAD, halves), :]
        + padded[0, pl.ds(PAD + 1, halves), :]
        + padded[2, pl.ds(PAD - 1, halves), :]
    )

    for offset in range(groups):
        share_copy(offset).wait_send()


def solution(mesh):
    groups, count = mesh.shape["src"], mesh.shape["space"]

    def step(adjoint_source, forward_field, medium, plane_map, depth, rough):
        parts, planes, rows, cells = adjoint_source.shape[1:]
        halves = rows // 2
        tall = rows + 2 * PAD
        slots = HIGH - LOW + 1
        f32 = jnp.float32
        dma = pltpu.SemaphoreType.DMA
        return pl.pallas_call(
            functools.partial(kernel, groups, count),
            out_shape=jax.ShapeDtypeStruct((1, halves, cells), f32),
            in_specs=[pl.BlockSpec(memory_space=pltpu.HBM)] * 6,
            out_specs=pl.BlockSpec(memory_space=pltpu.VMEM),
            scratch_shapes=[
                pltpu.VMEM((parts, planes, rows, cells), f32),
                pltpu.VMEM((parts, planes, rows, cells), jnp.bfloat16),
                pltpu.VMEM((2, planes, rows, cells), f32),
                pltpu.VMEM((planes, rows), jnp.int32),
                pltpu.VMEM((planes, rows), jnp.int32),
                pltpu.VMEM((9, halves, cells), f32),
                pltpu.VMEM((planes, rows, cells), f32),
                pltpu.VMEM((SWEEPS, planes + 1, 6, tall, cells), f32),
                pltpu.VMEM((SWEEPS - 1, planes + 1, 6, tall, cells), f32),
                pltpu.VMEM((planes, 2, tall, cells), f32),
                pltpu.VMEM((planes, rows, cells), f32),
                pltpu.VMEM((planes, rows, cells), f32),
                pltpu.VMEM((planes + 1, rows, cells), f32),
                pltpu.VMEM((planes + 1, rows, cells), f32),
                pltpu.VMEM((8, 128), f32),
                pltpu.VMEM((8, 128), f32),
                pltpu.VMEM((slots, rows, cells), f32),
                pltpu.VMEM((slots, halves, cells), f32),
                pltpu.VMEM((slots, halves, cells), f32),
                pltpu.VMEM((halves, cells), f32),
                pltpu.VMEM((groups, halves, cells), f32),
                pltpu.VMEM((3, halves + 2 * PAD, cells), f32),
                dma((planes,)),
                dma((planes,)),
                dma((4,)),
                dma((SWEEPS - 1, 2, PIECES)),
                dma((SWEEPS - 1, 2, PIECES)),
                dma((2,)),
                dma((slots,)),
                dma((slots,)),
                dma((groups,)),
                dma((groups,)),
            ],
            compiler_params=pltpu.CompilerParams(
                collective_id=0, has_side_effects=True, vmem_limit_bytes=48 * 1024 * 1024
            ),
            name="gradient",
        )(*(pltpu.with_memory_space_constraint(given, pltpu.HBM) for given in (adjoint_source, forward_field, medium, plane_map, depth, rough)))

    in_specs = (
        P("src", None, "space", None, None),
        P("src", None, "space", None, None),
        P(None, "space", None, None),
        P("space", None),
        P("src", "space", None),
        P(None, "space", None, None),
    )
    out_specs = P("space", None, None)
    return jax.shard_map(step, mesh=mesh, in_specs=in_specs, out_specs=out_specs, check_vma=False)
```

```python
import functools

import jax
import jax.numpy as jnp
from jax import lax
from jax.experimental import pallas as pl
from jax.experimental.pallas import tpu as pltpu
from jax.sharding import PartitionSpec as P

MESH = pl.DeviceIdType.MESH
SWEEPS = 4
REACH = 2
STEPS = (0.323, 1.658, 0.422, 0.752)
PAD = 8
BLOCK = 16
PIECES = 4
LOW, HIGH = -REACH - 1, REACH


def kernel(
    groups, count,
    source_hbm, saved_hbm, medium_hbm, map_hbm, depth_hbm, rough_hbm,
    out_ref,
    source, saved, mass, plane_map, depth, rough,
    inverse, field, mixed, part, upper, lower, where_to, how_deep, edge_out, edge_in,
    window, sent, landed, total, shares, padded,
    source_sem, mass_sem, load_sem, halo_send, halo_recv, edge_sem, window_send, window_recv, share_send, share_recv,
):
    planes, rows, cells = source.shape[1:]
    group = lax.axis_index("src")
    me = lax.axis_index("space")
    core = lax.rem(me, 2)
    has_below, has_above = me > 0, me < count - 1
    blocks = range(0, rows, BLOCK)
    lane = lax.broadcasted_iota(jnp.int32, (BLOCK, cells), 1)
    first_lane, last_lane = lane == 0, lane == cells - 1

    def at(start):
        return pl.ds(PAD + start, BLOCK)

    def ahead(value):
        return jnp.where(last_lane, 0.0, pltpu.roll(value, cells - 1, 1))

    def behind(value):
        return jnp.where(first_lane, 0.0, pltpu.roll(value, 1, 1))

    def present(offset):
        other = me + offset
        return (other >= 0) & (other < count)

    across = 1 - 2 * core
    even = core == 0

    barrier = pltpu.get_barrier_semaphore()
    for low, high in ((1, 1), (-1, -1), (2, 2), (3, -2), (4, -3)):
        offset = jnp.where(even, low, high)

        @pl.when(present(offset))
        def _():
            pl.semaphore_signal(barrier, inc=1, device_id={"space": me + offset}, device_id_type=MESH)
    for offset in range(1, groups):
        pl.semaphore_signal(
            barrier, inc=1,
            device_id={"src": lax.rem(group + offset, groups), "space": me + across},
            device_id_type=MESH,
        )
    awaited = groups - 1
    for low, high in ((1, 1), (-1, -1), (-2, -2), (-4, 2), (3, -3)):
        awaited = awaited + present(jnp.where(even, low, high)).astype(jnp.int32)

    def load_source(p):
        return pltpu.make_async_copy(source_hbm.at[0, :, p], source.at[:, p], source_sem.at[p])

    def load_mass(p):
        return pltpu.make_async_copy(medium_hbm.at[:, p], mass.at[:, p], mass_sem.at[p])

    for p in (0, planes - 1, *range(1, planes - 1)):
        load_source(p).start()
        load_mass(p).start()
    load_depth = pltpu.make_async_copy(depth_hbm.at[0], depth, load_sem.at[0])
    load_map = pltpu.make_async_copy(map_hbm, plane_map, load_sem.at[1])
    load_saved = pltpu.make_async_copy(saved_hbm.at[0], saved, load_sem.at[2])
    load_rough = pltpu.make_async_copy(rough_hbm.at[:, 0], rough, load_sem.at[3])
    for load in (load_depth, load_map, load_saved, load_rough):
        load.start()

    margin = jnp.zeros((PAD, cells), jnp.float32)
    for k in range(SWEEPS - 1):
        for p in range(planes):
            for c in (0, 1, 4, 5):
                field[k, p, c, pl.ds(PAD + rows, PAD), :] = margin
            for c in (2, 3):
                field[k, p + 1, c, pl.ds(0, PAD), :] = margin
                mixed[k, p + 1, c, pl.ds(0, PAD), :] = margin
            for c in (4, 5):
                mixed[k, p + 1, c, pl.ds(0, PAD), :] = margin
    for p in range(planes):
        for c in (0, 1):
            part[p, c, pl.ds(PAD + rows, PAD), :] = margin
    padded[...] = jnp.zeros_like(padded)

    @pl.when(jnp.logical_not(has_below))
    def _():
        for k in range(SWEEPS - 1):
            mixed[k, 0] = jnp.zeros(mixed.shape[2:], jnp.float32)
        edge_in[...] = jnp.full(edge_in.shape, -1000.0, jnp.float32)

    @pl.when(jnp.logical_not(has_above))
    def _():
        for k in range(SWEEPS - 1):
            field[k, planes, 2:6] = jnp.zeros((4, *field.shape[3:]), jnp.float32)

    piece = rows // PIECES

    def rows_of(q):
        return pl.ds(PAD + q * piece, piece)

    def halo_down(k, q):
        return pltpu.make_async_remote_copy(
            src_ref=field.at[k, 0, 2:6, rows_of(q)],
            dst_ref=field.at[k, planes, 2:6, rows_of(q)],
            send_sem=halo_send.at[k, 0, q],
            recv_sem=halo_recv.at[k, 0, q],
            device_id={"space": me - 1},
            device_id_type=MESH,
        )

    def halo_up(k, q):
        return pltpu.make_async_remote_copy(
            src_ref=mixed.at[k, planes, 0:4, rows_of(q)],
            dst_ref=mixed.at[k, 0, 0:4, rows_of(q)],
            send_sem=halo_send.at[k, 1, q],
            recv_sem=halo_recv.at[k, 1, q],
            device_id={"space": me + 1},
            device_id_type=MESH,
        )

    edge_up = pltpu.make_async_remote_copy(
        src_ref=edge_out,
        dst_ref=edge_in,
        send_sem=edge_sem.at[0],
        recv_sem=edge_sem.at[1],
        device_id={"space": me + 1},
        device_id_type=MESH,
    )

    def combine(k, p, span=blocks):
        for r in span:
            for i in (0, 1):
                x, y, z = (field[k, p, 2 * c + i, at(r), :] for c in range(3))
                x_next, z_next = (field[k, p, 2 * c + i, at(r + 1), :] for c in (0, 2))
                mixed[k, p + 1, i, at(r), :] = (ahead(x) - x) + z
                mixed[k, p + 1, 2 + i, at(r), :] = y + (x_next - x)
                mixed[k, p + 1, 4 + i, at(r), :] = (z_next - z) - (ahead(y) - y)

    def begin(p):
        load_source(p).wait()
        load_mass(p).wait()
        for r in blocks:
            span = pl.ds(r, BLOCK)
            turned = 1.0 / (4.0 + mass[0, p, span, :])
            inverse[p, span, :] = turned
            turned = STEPS[0] * turned
            for c in range(3):
                for i in (0, 1):
                    field[0, p, 2 * c + i, at(r), :] = source[c + 3 * i, p, span, :] * turned
        combine(0, p)

    def update(k, p, weight, span_of=blocks):
        before = k - 1
        inside = jnp.where((me == 0) & (p == 0), 0.0, 1.0).astype(jnp.float32)
        for r in span_of:
            span = pl.ds(r, BLOCK)
            real, imag = mass[0, p, span, :], mass[1, p, span, :]
            scale = weight * inverse[p, span, :]
            images, centers = [], []
            for i in (0, 1):
                x, y, z = (field[before, p, 2 * c + i, at(r), :] for c in range(3))
                y_up = field[before, p + 1, 2 + i, at(r), :]
                z_up = field[before, p + 1, 4 + i, at(r), :]
                curl_x = mixed[before, p + 1, 4 + i, at(r), :]
                curl_y = mixed[before, p + 1, i, at(r), :] - z_up
                curl_z = y_up - mixed[before, p + 1, 2 + i, at(r), :]
                curl_x_left = mixed[before, p + 1, 4 + i, at(r - 1), :]
                curl_z_left = field[before, p + 1, 2 + i, at(r - 1), :] - mixed[before, p + 1, 2 + i, at(r - 1), :]
                curl_y_low = (mixed[before, p, i, at(r), :] - z) * inside
                curl_z_low = (y - mixed[before, p, 2 + i, at(r), :]) * inside
                images.append((
                    (behind(curl_y) - curl_y) - (curl_z_left - curl_z),
                    (curl_z_low - curl_z) - (behind(curl_x) - curl_x),
                    (curl_x_left - curl_x) - (curl_y_low - curl_y),
                ))
                centers.append((x, y, z))
            for c in range(3):
                e_r, e_i = centers[0][c], centers[1][c]
                res_r = source[c, p, span, :] - (images[0][c] + real * e_r - imag * e_i)
                res_i = source[c + 3, p, span, :] - (images[1][c] + real * e_i + imag * e_r)
                field[k, p, 2 * c, at(r), :] = e_r + scale * res_r
                field[k, p, 2 * c + 1, at(r), :] = e_i + scale * res_i

    def products(p, span_of=blocks):
        for r in span_of:
            span = pl.ds(r, BLOCK)
            m = []
            for c in range(3):
                f_r = saved[c, p, span, :].astype(jnp.float32)
                f_i = saved[c + 3, p, span, :].astype(jnp.float32)
                a_r = field[SWEEPS - 1, p, 2 * c, at(r), :]
                a_i = field[SWEEPS - 1, p, 2 * c + 1, at(r), :]
                m.append(0.25 * (f_r * a_i + f_i * a_r))
            part[p, 0, at(r), :] = m[0] + ahead(m[0])
            part[p, 1, at(r), :] = m[2]
            lower[p, span, :] = m[1] + ahead(m[1])

    def averages(p, span_of=blocks):
        for r in span_of:
            span = pl.ds(r, BLOCK)
            shared = lower[p, span, :] + (part[p, 1, at(r), :] + part[p, 1, at(r + 1), :])
            lower[p, span, :] = shared
            upper[p, span, :] = shared + (part[p, 0, at(r), :] + part[p, 0, at(r + 1), :])

    place = lane.astype(jnp.float32)
    origin = me.astype(jnp.float32)
    halves = rows // 2
    slots = range(HIGH - LOW + 1)

    def window_sums(r):
        span = pl.ds(r, BLOCK)
        kept, targets = [], []
        for p in range(planes + 1):
            if p == planes:
                value = lower[0, span, :]
            elif p == planes - 1:
                value = upper[p, span, :]
            else:
                value = upper[p, span, :] + lower[p + 1, span, :]
            kept.append(jnp.where(place < how_deep[p, span, :], value, 0.0))
            targets.append(where_to[p, span, :] - origin)
        for slot in slots:
            offset = slot + LOW
            terms = [p for p in range(planes + 1) if (p == planes and offset < HIGH) or (p < planes and offset > LOW)]
            sum_here = jnp.zeros((BLOCK, cells), jnp.float32)
            for p in terms:
                sum_here = sum_here + jnp.where(targets[p] == float(offset), kept[p], 0.0)
            window[slot, span, :] = sum_here
            folded = window[slot, pl.ds(r, BLOCK // 2, stride=2), :] + window[slot, pl.ds(r + 1, BLOCK // 2, stride=2), :]
            sent[slot, pl.ds(r // 2, BLOCK // 2), :] = folded

    def outer(t, carry):
        begin(jnp.where(t == core, 0, planes - 1))
        return carry

    lax.fori_loop(0, 2, outer, 0)
    pl.semaphore_wait(barrier, awaited)

    @pl.when(has_below)
    def _():
        for q in range(PIECES):
            halo_down(0, q).start()

    @pl.when(has_above)
    def _():
        for q in range(PIECES):
            halo_up(0, q).start()

    def inner(p, carry):
        begin(p)
        return carry

    lax.fori_loop(1, planes - 1, inner, 0)

    load_depth.wait()
    load_map.wait()
    edge_out[...] = jnp.zeros_like(edge_out)
    edge_out[0:1, 0:rows] = depth[planes - 1:planes, :].astype(jnp.float32)
    edge_out[1:2, 0:rows] = plane_map[planes - 1:planes, :].astype(jnp.float32)

    @pl.when(has_above)
    def _():
        edge_up.start()

    diagonal = lax.broadcasted_iota(jnp.int32, (rows, rows), 0) == lax.broadcasted_iota(jnp.int32, (rows, rows), 1)

    def columns(row):
        spread = jnp.where(diagonal, jnp.broadcast_to(row, (rows, rows)), 0.0)
        return jnp.broadcast_to(jnp.sum(spread, axis=1, keepdims=True), (rows, cells))

    for p in range(planes):
        how_deep[p] = columns(depth[p:p + 1, :].astype(jnp.float32))
        where_to[p] = columns(plane_map[p:p + 1, :].astype(jnp.float32))

    def await_halo(k, p, q):
        @pl.when((p == 0) & has_below)
        def _():
            halo_up(k, q).wait_recv()

        @pl.when((p == planes - 1) & has_above)
        def _():
            halo_down(k, q).wait_recv()

    def blocks_of(q):
        return range(q * piece, (q + 1) * piece, BLOCK)

    def end_at(t):
        return jnp.where(t == core, planes - 1, 0)

    def complete_after(q):
        return [q - 1] * (q > 0) + [q] * (q == PIECES - 1)

    def turn(k, carry):
        weight = jnp.where(k == 1, STEPS[1], STEPS[2]).astype(jnp.float32)

        def middle(p, carry):
            update(k, p, weight)
            combine(k, p)
            return carry

        lax.fori_loop(1, planes - 1, middle, 0)

        for q in range(PIECES):
            def ends(t, carry):
                p = end_at(t)
                await_halo(k - 1, p, q)
                update(k, p, weight, blocks_of(q))

                @pl.when((p == 0) & has_below)
                def _():
                    halo_down(k, q).start()

                for ready in complete_after(q):
                    combine(k, p, blocks_of(ready))

                    @pl.when((p == planes - 1) & has_above)
                    def _():
                        halo_up(k, ready).start()

                return carry

            lax.fori_loop(0, 2, ends, 0)
        return carry

    lax.fori_loop(1, SWEEPS - 1, turn, 0)

    last = SWEEPS - 1
    load_saved.wait()

    def middle(p, carry):
        update(last, p, STEPS[last])
        products(p)
        averages(p)
        return carry

    lax.fori_loop(1, planes - 1, middle, 0)

    @pl.when(has_above)
    def _():
        edge_up.wait_send()

    @pl.when(has_below)
    def _():
        edge_up.wait_recv()

    how_deep[planes] = columns(edge_in[0:1, 0:rows])
    where_to[planes] = columns(edge_in[1:2, 0:rows])

    for q in range(PIECES):
        def ends(t, carry):
            p = end_at(t)
            await_halo(last - 1, p, q)
            update(last, p, STEPS[last], blocks_of(q))
            products(p, blocks_of(q))
            for ready in complete_after(q):
                averages(p, blocks_of(ready))
            return carry

        lax.fori_loop(0, 2, ends, 0)
        for ready in complete_after(q):
            for r in blocks_of(ready):
                window_sums(r)

    def window_copy(slot):
        offset = slot + LOW
        return pltpu.make_async_remote_copy(
            src_ref=sent.at[slot],
            dst_ref=landed.at[slot],
            send_sem=window_send.at[slot],
            recv_sem=window_recv.at[slot],
            device_id={"space": me + offset + (across if offset % 2 == 0 else -across)},
            device_id_type=MESH,
        )

    def leaves(slot):
        offset = slot + LOW
        return present(offset) & (offset != across)

    def lands(slot):
        offset = slot + LOW
        return present(across - offset) & (offset != across)

    farthest_first = sorted(slots, key=lambda slot: -abs(slot + LOW))
    for slot in farthest_first:
        @pl.when(leaves(slot))
        def _():
            window_copy(slot).start()

    total[...] = sent[across - LOW]
    for slot in farthest_first[::-1]:
        @pl.when(lands(slot))
        def _():
            window_copy(slot).wait_recv()
            total[...] += landed[slot]

    def share_copy(offset):
        return pltpu.make_async_remote_copy(
            src_ref=total,
            dst_ref=shares.at[group],
            send_sem=share_send.at[offset],
            recv_sem=share_recv.at[offset],
            device_id={"src": lax.rem(group + offset, groups), "space": me + across},
            device_id_type=MESH,
        )

    def share_from(offset):
        return pltpu.make_async_remote_copy(
            src_ref=total,
            dst_ref=shares.at[lax.rem(group + groups - offset, groups)],
            send_sem=share_send.at[offset],
            recv_sem=share_recv.at[offset],
            device_id={"src": lax.rem(group + offset, groups), "space": me + across},
            device_id_type=MESH,
        )

    for offset in sorted(range(groups), key=lambda offset: -min(offset, groups - offset)):
        share_copy(offset).start()

    for k in range(SWEEPS - 1):
        @pl.when(has_below)
        def _():
            for q in range(PIECES):
                halo_down(k, q).wait_send()

        @pl.when(has_above)
        def _():
            for q in range(PIECES):
                halo_up(k, q).wait_send()
    for slot in slots:
        @pl.when(leaves(slot))
        def _():
            window_copy(slot).wait_send()
    load_rough.wait()
    for offset in range(groups):
        share_from(offset).wait_recv()
    whole = shares[0]
    for slot in range(1, groups):
        whole = whole + shares[slot]

    lanes = lax.broadcasted_iota(jnp.int32, (halves, cells), 1)
    for a in range(3):
        left, middle, right = (rough[3 * a + b] * whole for b in range(3))
        row_sum = middle
        row_sum = row_sum + jnp.where(lanes == cells - 1, 0.0, pltpu.roll(left, cells - 1, 1))
        row_sum = row_sum + jnp.where(lanes == 0, 0.0, pltpu.roll(right, 1, 1))
        padded[a, pl.ds(PAD, halves), :] = row_sum
    out_ref[0] = (
        padded[1, pl.ds(PAD, halves), :]
        + padded[0, pl.ds(PAD + 1, halves), :]
        + padded[2, pl.ds(PAD - 1, halves), :]
    )

    for offset in range(groups):
        share_copy(offset).wait_send()


def solution(mesh):
    groups, count = mesh.shape["src"], mesh.shape["space"]

    def step(adjoint_source, forward_field, medium, plane_map, depth, rough):
        parts, planes, rows, cells = adjoint_source.shape[1:]
        halves = rows // 2
        tall = rows + 2 * PAD
        slots = HIGH - LOW + 1
        f32 = jnp.float32
        dma = pltpu.SemaphoreType.DMA
        return pl.pallas_call(
            functools.partial(kernel, groups, count),
            out_shape=jax.ShapeDtypeStruct((1, halves, cells), f32),
            in_specs=[pl.BlockSpec(memory_space=pltpu.HBM)] * 6,
            out_specs=pl.BlockSpec(memory_space=pltpu.VMEM),
            scratch_shapes=[
                pltpu.VMEM((parts, planes, rows, cells), f32),
                pltpu.VMEM((parts, planes, rows, cells), jnp.bfloat16),
                pltpu.VMEM((2, planes, rows, cells), f32),
                pltpu.VMEM((planes, rows), jnp.int32),
                pltpu.VMEM((planes, rows), jnp.int32),
                pltpu.VMEM((9, halves, cells), f32),
                pltpu.VMEM((planes, rows, cells), f32),
                pltpu.VMEM((SWEEPS, planes + 1, 6, tall, cells), f32),
                pltpu.VMEM((SWEEPS - 1, planes + 1, 6, tall, cells), f32),
                pltpu.VMEM((planes, 2, tall, cells), f32),
                pltpu.VMEM((planes, rows, cells), f32),
                pltpu.VMEM((planes, rows, cells), f32),
                pltpu.VMEM((planes + 1, rows, cells), f32),
                pltpu.VMEM((planes + 1, rows, cells), f32),
                pltpu.VMEM((8, 128), f32),
                pltpu.VMEM((8, 128), f32),
                pltpu.VMEM((slots, rows, cells), f32),
                pltpu.VMEM((slots, halves, cells), f32),
                pltpu.VMEM((slots, halves, cells), f32),
                pltpu.VMEM((halves, cells), f32),
                pltpu.VMEM((groups, halves, cells), f32),
                pltpu.VMEM((3, halves + 2 * PAD, cells), f32),
                dma((planes,)),
                dma((planes,)),
                dma((4,)),
                dma((SWEEPS - 1, 2, PIECES)),
                dma((SWEEPS - 1, 2, PIECES)),
                dma((2,)),
                dma((slots,)),
                dma((slots,)),
                dma((groups,)),
                dma((groups,)),
            ],
            compiler_params=pltpu.CompilerParams(
                collective_id=0, has_side_effects=True, vmem_limit_bytes=48 * 1024 * 1024
            ),
            name="gradient",
        )(*(pltpu.with_memory_space_constraint(given, pltpu.HBM) for given in (adjoint_source, forward_field, medium, plane_map, depth, rough)))

    in_specs = (
        P("src", None, "space", None, None),
        P("src", None, "space", None, None),
        P(None, "space", None, None),
        P("space", None),
        P("src", "space", None),
        P(None, "space", None, None),
    )
    out_specs = P("space", None, None)
    return jax.shard_map(step, mesh=mesh, in_specs=in_specs, out_specs=out_specs, check_vma=False)
```

```python
import functools

import jax
import jax.numpy as jnp
from jax import lax
from jax.experimental import pallas as pl
from jax.experimental.pallas import tpu as pltpu
from jax.sharding import PartitionSpec as P

MESH = pl.DeviceIdType.MESH
SWEEPS = 4
REACH = 2
STEPS = (0.323, 1.658, 0.422, 0.752)
PAD = 8
BLOCK = 16
PIECES = 4
PARTS = 1
LOW, HIGH = -REACH - 1, REACH


def kernel(
    groups, count,
    source_hbm, saved_hbm, medium_hbm, map_hbm, depth_hbm, rough_hbm,
    out_ref,
    source, saved, mass, plane_map, depth, rough,
    inverse, field, mixed, part, upper, lower, where_to, how_deep, edge_out, edge_in,
    window, sent, landed, total, shares, padded,
    source_sem, mass_sem, load_sem, halo_send, halo_recv, edge_sem, window_send, window_recv, share_send, share_recv,
):
    planes, rows, cells = source.shape[1:]
    group = lax.axis_index("src")
    me = lax.axis_index("space")
    core = lax.rem(me, 2)
    has_below, has_above = me > 0, me < count - 1
    blocks = range(0, rows, BLOCK)
    lane = lax.broadcasted_iota(jnp.int32, (BLOCK, cells), 1)
    first_lane, last_lane = lane == 0, lane == cells - 1

    def at(start):
        return pl.ds(PAD + start, BLOCK)

    def ahead(value):
        return jnp.where(last_lane, 0.0, pltpu.roll(value, cells - 1, 1))

    def behind(value):
        return jnp.where(first_lane, 0.0, pltpu.roll(value, 1, 1))

    def present(offset):
        other = me + offset
        return (other >= 0) & (other < count)

    barrier = pltpu.get_barrier_semaphore()
    awaited = groups - 1
    for offset in (1, -1, 2, -2, 3):
        @pl.when(present(offset))
        def _():
            pl.semaphore_signal(barrier, inc=1, device_id={"space": me + offset}, device_id_type=MESH)
    for offset in range(1, groups):
        pl.semaphore_signal(barrier, inc=1, device_id={"src": lax.rem(group + offset, groups)}, device_id_type=MESH)
    for offset in range(LOW, HIGH + 1):
        if offset != 0:
            awaited = awaited + present(offset).astype(jnp.int32)

    def load_source(p):
        return pltpu.make_async_copy(source_hbm.at[0, :, p], source.at[:, p], source_sem.at[p])

    def load_mass(p):
        return pltpu.make_async_copy(medium_hbm.at[:, p], mass.at[:, p], mass_sem.at[p])

    for p in (0, planes - 1, *range(1, planes - 1)):
        load_source(p).start()
        load_mass(p).start()
    load_depth = pltpu.make_async_copy(depth_hbm.at[0], depth, load_sem.at[0])
    load_map = pltpu.make_async_copy(map_hbm, plane_map, load_sem.at[1])
    load_saved = pltpu.make_async_copy(saved_hbm.at[0], saved, load_sem.at[2])
    load_rough = pltpu.make_async_copy(rough_hbm.at[:, 0], rough, load_sem.at[3])
    for load in (load_depth, load_map, load_saved, load_rough):
        load.start()

    margin = jnp.zeros((PAD, cells), jnp.float32)
    for k in range(SWEEPS - 1):
        for p in range(planes):
            for c in (0, 1, 4, 5):
                field[k, p, c, pl.ds(PAD + rows, PAD), :] = margin
            for c in (2, 3):
                field[k, p + 1, c, pl.ds(0, PAD), :] = margin
                mixed[k, p + 1, c, pl.ds(0, PAD), :] = margin
            for c in (4, 5):
                mixed[k, p + 1, c, pl.ds(0, PAD), :] = margin
    for p in range(planes):
        for c in (0, 1):
            part[p, c, pl.ds(PAD + rows, PAD), :] = margin
    padded[...] = jnp.zeros_like(padded)

    @pl.when(jnp.logical_not(has_below))
    def _():
        for k in range(SWEEPS - 1):
            mixed[k, 0] = jnp.zeros(mixed.shape[2:], jnp.float32)
        edge_in[...] = jnp.full(edge_in.shape, -1000.0, jnp.float32)

    @pl.when(jnp.logical_not(has_above))
    def _():
        for k in range(SWEEPS - 1):
            field[k, planes, 2:6] = jnp.zeros((4, *field.shape[3:]), jnp.float32)

    piece = rows // PIECES

    def rows_of(q):
        return pl.ds(PAD + q * piece, piece)

    def halo_down(k, q):
        return pltpu.make_async_remote_copy(
            src_ref=field.at[k, 0, 2:6, rows_of(q)],
            dst_ref=field.at[k, planes, 2:6, rows_of(q)],
            send_sem=halo_send.at[k, 0, q],
            recv_sem=halo_recv.at[k, 0, q],
            device_id={"space": me - 1},
            device_id_type=MESH,
        )

    def halo_up(k, q):
        return pltpu.make_async_remote_copy(
            src_ref=mixed.at[k, planes, 0:4, rows_of(q)],
            dst_ref=mixed.at[k, 0, 0:4, rows_of(q)],
            send_sem=halo_send.at[k, 1, q],
            recv_sem=halo_recv.at[k, 1, q],
            device_id={"space": me + 1},
            device_id_type=MESH,
        )

    edge_up = pltpu.make_async_remote_copy(
        src_ref=edge_out,
        dst_ref=edge_in,
        send_sem=edge_sem.at[0],
        recv_sem=edge_sem.at[1],
        device_id={"space": me + 1},
        device_id_type=MESH,
    )

    def combine(k, p, span=blocks):
        for r in span:
            for i in (0, 1):
                x, y, z = (field[k, p, 2 * c + i, at(r), :] for c in range(3))
                x_next, z_next = (field[k, p, 2 * c + i, at(r + 1), :] for c in (0, 2))
                mixed[k, p + 1, i, at(r), :] = (ahead(x) - x) + z
                mixed[k, p + 1, 2 + i, at(r), :] = y + (x_next - x)
                mixed[k, p + 1, 4 + i, at(r), :] = (z_next - z) - (ahead(y) - y)

    def begin(p):
        load_source(p).wait()
        load_mass(p).wait()
        for r in blocks:
            span = pl.ds(r, BLOCK)
            turned = 1.0 / (4.0 + mass[0, p, span, :])
            inverse[p, span, :] = turned
            turned = STEPS[0] * turned
            for c in range(3):
                for i in (0, 1):
                    field[0, p, 2 * c + i, at(r), :] = source[c + 3 * i, p, span, :] * turned
        combine(0, p)

    def update(k, p, weight, span_of=blocks):
        before = k - 1
        inside = jnp.where((me == 0) & (p == 0), 0.0, 1.0).astype(jnp.float32)
        for r in span_of:
            span = pl.ds(r, BLOCK)
            real, imag = mass[0, p, span, :], mass[1, p, span, :]
            scale = weight * inverse[p, span, :]
            images, centers = [], []
            for i in (0, 1):
                x, y, z = (field[before, p, 2 * c + i, at(r), :] for c in range(3))
                y_up = field[before, p + 1, 2 + i, at(r), :]
                z_up = field[before, p + 1, 4 + i, at(r), :]
                curl_x = mixed[before, p + 1, 4 + i, at(r), :]
                curl_y = mixed[before, p + 1, i, at(r), :] - z_up
                curl_z = y_up - mixed[before, p + 1, 2 + i, at(r), :]
                curl_x_left = mixed[before, p + 1, 4 + i, at(r - 1), :]
                curl_z_left = field[before, p + 1, 2 + i, at(r - 1), :] - mixed[before, p + 1, 2 + i, at(r - 1), :]
                curl_y_low = (mixed[before, p, i, at(r), :] - z) * inside
                curl_z_low = (y - mixed[before, p, 2 + i, at(r), :]) * inside
                images.append((
                    (behind(curl_y) - curl_y) - (curl_z_left - curl_z),
                    (curl_z_low - curl_z) - (behind(curl_x) - curl_x),
                    (curl_x_left - curl_x) - (curl_y_low - curl_y),
                ))
                centers.append((x, y, z))
            for c in range(3):
                e_r, e_i = centers[0][c], centers[1][c]
                res_r = source[c, p, span, :] - (images[0][c] + real * e_r - imag * e_i)
                res_i = source[c + 3, p, span, :] - (images[1][c] + real * e_i + imag * e_r)
                field[k, p, 2 * c, at(r), :] = e_r + scale * res_r
                field[k, p, 2 * c + 1, at(r), :] = e_i + scale * res_i

    def products(p, span_of=blocks):
        for r in span_of:
            span = pl.ds(r, BLOCK)
            m = []
            for c in range(3):
                f_r = saved[c, p, span, :].astype(jnp.float32)
                f_i = saved[c + 3, p, span, :].astype(jnp.float32)
                a_r = field[SWEEPS - 1, p, 2 * c, at(r), :]
                a_i = field[SWEEPS - 1, p, 2 * c + 1, at(r), :]
                m.append(0.25 * (f_r * a_i + f_i * a_r))
            part[p, 0, at(r), :] = m[0] + ahead(m[0])
            part[p, 1, at(r), :] = m[2]
            lower[p, span, :] = m[1] + ahead(m[1])

    def averages(p, span_of=blocks):
        for r in span_of:
            span = pl.ds(r, BLOCK)
            shared = lower[p, span, :] + (part[p, 1, at(r), :] + part[p, 1, at(r + 1), :])
            lower[p, span, :] = shared
            upper[p, span, :] = shared + (part[p, 0, at(r), :] + part[p, 0, at(r + 1), :])

    place = lane.astype(jnp.float32)
    origin = me.astype(jnp.float32)
    halves = rows // 2
    slots = range(HIGH - LOW + 1)

    def window_sums(r):
        span = pl.ds(r, BLOCK)
        kept, targets = [], []
        for p in range(planes + 1):
            if p == planes:
                value = lower[0, span, :]
            elif p == planes - 1:
                value = upper[p, span, :]
            else:
                value = upper[p, span, :] + lower[p + 1, span, :]
            kept.append(jnp.where(place < how_deep[p, span, :], value, 0.0))
            targets.append(where_to[p, span, :] - origin)
        for slot in slots:
            offset = slot + LOW
            terms = [p for p in range(planes + 1) if (p == planes and offset < HIGH) or (p < planes and offset > LOW)]
            sum_here = jnp.zeros((BLOCK, cells), jnp.float32)
            for p in terms:
                sum_here = sum_here + jnp.where(targets[p] == float(offset), kept[p], 0.0)
            window[slot, span, :] = sum_here
            folded = window[slot, pl.ds(r, BLOCK // 2, stride=2), :] + window[slot, pl.ds(r + 1, BLOCK // 2, stride=2), :]
            sent[slot, pl.ds(r // 2, BLOCK // 2), :] = folded

    def outer(t, carry):
        begin(jnp.where(t == core, 0, planes - 1))
        return carry

    lax.fori_loop(0, 2, outer, 0)
    pl.semaphore_wait(barrier, awaited)

    @pl.when(has_below)
    def _():
        for q in range(PIECES):
            halo_down(0, q).start()

    @pl.when(has_above)
    def _():
        for q in range(PIECES):
            halo_up(0, q).start()

    def inner(p, carry):
        begin(p)
        return carry

    lax.fori_loop(1, planes - 1, inner, 0)

    load_depth.wait()
    load_map.wait()
    edge_out[...] = jnp.zeros_like(edge_out)
    edge_out[0:1, 0:rows] = depth[planes - 1:planes, :].astype(jnp.float32)
    edge_out[1:2, 0:rows] = plane_map[planes - 1:planes, :].astype(jnp.float32)

    @pl.when(has_above)
    def _():
        edge_up.start()

    diagonal = lax.broadcasted_iota(jnp.int32, (rows, rows), 0) == lax.broadcasted_iota(jnp.int32, (rows, rows), 1)

    def columns(row):
        spread = jnp.where(diagonal, jnp.broadcast_to(row, (rows, rows)), 0.0)
        return jnp.broadcast_to(jnp.sum(spread, axis=1, keepdims=True), (rows, cells))

    for p in range(planes):
        how_deep[p] = columns(depth[p:p + 1, :].astype(jnp.float32))
        where_to[p] = columns(plane_map[p:p + 1, :].astype(jnp.float32))

    def await_halo(k, p, q):
        @pl.when((p == 0) & has_below)
        def _():
            halo_up(k, q).wait_recv()

        @pl.when((p == planes - 1) & has_above)
        def _():
            halo_down(k, q).wait_recv()

    def blocks_of(q):
        return range(q * piece, (q + 1) * piece, BLOCK)

    def end_at(t):
        return jnp.where(t == core, planes - 1, 0)

    def complete_after(q):
        return [q - 1] * (q > 0) + [q] * (q == PIECES - 1)

    def turn(k, carry):
        weight = jnp.where(k == 1, STEPS[1], STEPS[2]).astype(jnp.float32)

        def middle(p, carry):
            update(k, p, weight)
            combine(k, p)
            return carry

        lax.fori_loop(1, planes - 1, middle, 0)

        for q in range(PIECES):
            def ends(t, carry):
                p = end_at(t)
                await_halo(k - 1, p, q)
                update(k, p, weight, blocks_of(q))

                @pl.when((p == 0) & has_below)
                def _():
                    halo_down(k, q).start()

                for ready in complete_after(q):
                    combine(k, p, blocks_of(ready))

                    @pl.when((p == planes - 1) & has_above)
                    def _():
                        halo_up(k, ready).start()

                return carry

            lax.fori_loop(0, 2, ends, 0)
        return carry

    lax.fori_loop(1, SWEEPS - 1, turn, 0)

    last = SWEEPS - 1
    load_saved.wait()

    def middle(p, carry):
        update(last, p, STEPS[last])
        products(p)
        averages(p)
        return carry

    lax.fori_loop(1, planes - 1, middle, 0)

    @pl.when(has_above)
    def _():
        edge_up.wait_send()

    @pl.when(has_below)
    def _():
        edge_up.wait_recv()

    how_deep[planes] = columns(edge_in[0:1, 0:rows])
    where_to[planes] = columns(edge_in[1:2, 0:rows])

    share = halves // PARTS

    def lines(h):
        return pl.ds(h * share, share)

    def window_copy(slot, h):
        return pltpu.make_async_remote_copy(
            src_ref=sent.at[slot, lines(h)],
            dst_ref=landed.at[slot, lines(h)],
            send_sem=window_send.at[slot, h],
            recv_sem=window_recv.at[slot, h],
            device_id={"space": me + (slot + LOW)},
            device_id_type=MESH,
        )

    for q in range(PIECES):
        def ends(t, carry):
            p = end_at(t)
            await_halo(last - 1, p, q)
            update(last, p, STEPS[last], blocks_of(q))
            products(p, blocks_of(q))
            for ready in complete_after(q):
                averages(p, blocks_of(ready))
            return carry

        lax.fori_loop(0, 2, ends, 0)
        for ready in complete_after(q):
            for r in blocks_of(ready):
                window_sums(r)
            lines_done = (ready + 1) * piece // 2
            if lines_done % share == 0:
                for slot in sorted(slots, key=lambda slot: -abs(slot + LOW)):
                    if slot + LOW != 0:
                        @pl.when(present(slot + LOW))
                        def _():
                            window_copy(slot, lines_done // share - 1).start()

    def share_copy(offset, h):
        return pltpu.make_async_remote_copy(
            src_ref=shares.at[group, lines(h)],
            dst_ref=shares.at[group, lines(h)],
            send_sem=share_send.at[offset - 1, h],
            recv_sem=share_recv.at[offset - 1, h],
            device_id={"src": lax.rem(group + offset, groups)},
            device_id_type=MESH,
        )

    def share_from(offset, h):
        slot = lax.rem(group + groups - offset, groups)
        return pltpu.make_async_remote_copy(
            src_ref=shares.at[slot, lines(h)],
            dst_ref=shares.at[slot, lines(h)],
            send_sem=share_send.at[offset - 1, h],
            recv_sem=share_recv.at[offset - 1, h],
            device_id={"src": lax.rem(group + offset, groups)},
            device_id_type=MESH,
        )

    for h in range(PARTS):
        total[lines(h), :] = sent[-LOW, lines(h), :]
        for slot in sorted(slots, key=lambda slot: abs(slot + LOW)):
            if slot + LOW != 0:
                @pl.when(present(-(slot + LOW)))
                def _():
                    window_copy(slot, h).wait_recv()
                    total[lines(h), :] += landed[slot, lines(h), :]
        shares[group, lines(h), :] = total[lines(h), :]
        for offset in sorted(range(1, groups), key=lambda offset: -min(offset, groups - offset)):
            share_copy(offset, h).start()

    for k in range(SWEEPS - 1):
        @pl.when(has_below)
        def _():
            for q in range(PIECES):
                halo_down(k, q).wait_send()

        @pl.when(has_above)
        def _():
            for q in range(PIECES):
                halo_up(k, q).wait_send()
    for slot in slots:
        if slot + LOW != 0:
            @pl.when(present(slot + LOW))
            def _():
                for h in range(PARTS):
                    window_copy(slot, h).wait_send()
    load_rough.wait()
    for h in range(PARTS):
        for offset in range(1, groups):
            share_from(offset, h).wait_recv()
    whole = shares[0]
    for slot in range(1, groups):
        whole = whole + shares[slot]

    lanes = lax.broadcasted_iota(jnp.int32, (halves, cells), 1)
    for a in range(3):
        left, middle, right = (rough[3 * a + b] * whole for b in range(3))
        row_sum = middle
        row_sum = row_sum + jnp.where(lanes == cells - 1, 0.0, pltpu.roll(left, cells - 1, 1))
        row_sum = row_sum + jnp.where(lanes == 0, 0.0, pltpu.roll(right, 1, 1))
        padded[a, pl.ds(PAD, halves), :] = row_sum
    out_ref[0] = (
        padded[1, pl.ds(PAD, halves), :]
        + padded[0, pl.ds(PAD + 1, halves), :]
        + padded[2, pl.ds(PAD - 1, halves), :]
    )

    for h in range(PARTS):
        for offset in range(1, groups):
            share_copy(offset, h).wait_send()


def solution(mesh):
    groups, count = mesh.shape["src"], mesh.shape["space"]

    def step(adjoint_source, forward_field, medium, plane_map, depth, rough):
        parts, planes, rows, cells = adjoint_source.shape[1:]
        halves = rows // 2
        tall = rows + 2 * PAD
        slots = HIGH - LOW + 1
        f32 = jnp.float32
        dma = pltpu.SemaphoreType.DMA
        return pl.pallas_call(
            functools.partial(kernel, groups, count),
            out_shape=jax.ShapeDtypeStruct((1, halves, cells), f32),
            in_specs=[pl.BlockSpec(memory_space=pltpu.HBM)] * 6,
            out_specs=pl.BlockSpec(memory_space=pltpu.VMEM),
            scratch_shapes=[
                pltpu.VMEM((parts, planes, rows, cells), f32),
                pltpu.VMEM((parts, planes, rows, cells), jnp.bfloat16),
                pltpu.VMEM((2, planes, rows, cells), f32),
                pltpu.VMEM((planes, rows), jnp.int32),
                pltpu.VMEM((planes, rows), jnp.int32),
                pltpu.VMEM((9, halves, cells), f32),
                pltpu.VMEM((planes, rows, cells), f32),
                pltpu.VMEM((SWEEPS, planes + 1, 6, tall, cells), f32),
                pltpu.VMEM((SWEEPS - 1, planes + 1, 6, tall, cells), f32),
                pltpu.VMEM((planes, 2, tall, cells), f32),
                pltpu.VMEM((planes, rows, cells), f32),
                pltpu.VMEM((planes, rows, cells), f32),
                pltpu.VMEM((planes + 1, rows, cells), f32),
                pltpu.VMEM((planes + 1, rows, cells), f32),
                pltpu.VMEM((8, 128), f32),
                pltpu.VMEM((8, 128), f32),
                pltpu.VMEM((slots, rows, cells), f32),
                pltpu.VMEM((slots, halves, cells), f32),
                pltpu.VMEM((slots, halves, cells), f32),
                pltpu.VMEM((halves, cells), f32),
                pltpu.VMEM((groups, halves, cells), f32),
                pltpu.VMEM((3, halves + 2 * PAD, cells), f32),
                dma((planes,)),
                dma((planes,)),
                dma((4,)),
                dma((SWEEPS - 1, 2, PIECES)),
                dma((SWEEPS - 1, 2, PIECES)),
                dma((2,)),
                dma((slots, PARTS)),
                dma((slots, PARTS)),
                dma((groups - 1, PARTS)),
                dma((groups - 1, PARTS)),
            ],
            compiler_params=pltpu.CompilerParams(
                collective_id=0, has_side_effects=True, vmem_limit_bytes=48 * 1024 * 1024
            ),
            name="gradient",
        )(*(pltpu.with_memory_space_constraint(given, pltpu.HBM) for given in (adjoint_source, forward_field, medium, plane_map, depth, rough)))

    in_specs = (
        P("src", None, "space", None, None),
        P("src", None, "space", None, None),
        P(None, "space", None, None),
        P("space", None),
        P("src", "space", None),
        P(None, "space", None, None),
    )
    out_specs = P("space", None, None)
    return jax.shard_map(step, mesh=mesh, in_specs=in_specs, out_specs=out_specs, check_vma=False)
```
